32 devices in a mesh: req: 8 (over z, x), ctx: 4 (over y, core).
Axes of the slice: x: 2, y: 2, z: 4, core: 2. Of those that a mesh axis runs over, the one named last changes fastest.
Arguments:
- item_table: bfloat16 [16384, 256], P('req'), may hold values from -6 to 6
- cand_owner: int32 [8, 512, 1], P('req'), may hold values from 0 to 7; in each aligned block of 128 rows (0 to 127, 128 to 255, ..., all dimensions but the last counted through in order) at most 32 rows name the same one
- cand_slot: int32 [8, 512], P('req'), may hold values from 0 to 2047
- w_in: bfloat16 [256, 1024], replicated, may hold values from -0.375 to 0.375
- w_uq: bfloat16 [1024, 2048], replicated, may hold values from -0.1875 to 0.1875
- w_out: bfloat16 [1024, 1024], replicated, may hold values from -0.1875 to 0.1875
- k_cache: bfloat16 [8, 16384, 1024], P('req', 'ctx'), may hold values from -12 to 12
- v_cache: bfloat16 [8, 16384, 1024], P('req', 'ctx'), may hold values from -6 to 6
- hist_len: int32 [8], P('req'), may hold values from 1024 to 16384, as said below
Outputs:
- ranked: bfloat16 [8, 512, 1024], P('req', 'ctx')
The draws below stay inside these ranges and needn't reach their ends.
Inputs may be any that keep to these rules, and one draw needn't show every extreme that they name: `cand_owner`: in each aligned block of 512 / 4 candidates of a user, no owner is named more than 32 times, and in some block one owner is named exactly 32 times. `hist_len`: in every draw some user has the full 16384 events.
All inputs are finite; a program needn't handle non-finite values.
Results may differ from the reference program's by a relative error of at most 0.014.
Values may be sent and summed in bfloat16 or wider, within the bound.
No kernel may reach another device: no remote copies, remote signals or barrier semaphores. Data moves between devices by JAX's collectives and lax.ppermute only.
A program may use at most 128 MiB of HBM per device.

```python
import math
import jax
import jax.numpy as jnp
import numpy as np
from jax import lax

DM = 1024
HEADS = 8
DE = 256
CAND = 512
ITEMS_DEV = 2048
DH = 128
USERS = 8
HIST = 16384
ITEMS = 16384
CAP = 32
N_REQ = 8
N_CTX = 4


def draw_hist_len(key, part):
    key_lengths, key_chosen = jax.random.split(key)
    lengths = jax.random.randint(key_lengths, (USERS,), HIST // 16, HIST + 1)
    chosen = jax.random.randint(key_chosen, (), 0, USERS)
    return jnp.where(jnp.arange(USERS) == chosen, HIST, lengths).astype(jnp.int32)


def set_ends(result, stream_key, low, high):
    extent = result.shape
    place = [jax.random.randint(jax.random.fold_in(stream_key, axis), (), 0, extent[axis]) for axis in range(len(extent))]
    result = result.at[tuple(place)].set(low)
    longest = extent.index(max(extent))
    place[longest] = (place[longest] + 1) % extent[longest]
    return result.at[tuple(place)].set(high)


def level_of(stream_key, extent, shards, least, high):
    loudness, own = 1.0, jax.random.fold_in(stream_key, 6)
    for dim, blocks in shards:
        heights = jnp.exp(jax.random.uniform(jax.random.fold_in(own, dim), (blocks,), jnp.float32, least / len(shards), high / len(shards)))
        loudness = loudness * jnp.repeat(heights, extent[dim] // blocks).reshape([-1 if axis == dim else 1 for axis in range(len(extent))])
    return loudness


def routed_block(stream_key, own, number, rows, amount, top, limit, skew):
    sequence = jax.random.permutation(stream_key, amount)
    heavy_load, common = load_shares(amount, rows * top, limit, skew, True), load_shares(amount, rows * top, limit, skew, False)
    places = jnp.arange(amount)

    def named(tallies, rotation):
        used = int((tallies > 0).sum())
        fixed = max(1, used // 4)
        moved = fixed + (places - fixed + rotation * (used - fixed)) % max(1, amount - fixed)
        return jnp.zeros((amount,), jnp.int32).at[sequence[jnp.where(places < fixed, places, moved)]].set(jnp.asarray(tallies, jnp.int32))

    tallies = jnp.where(number % 4 == 0, named(heavy_load, number // 4), named(common, number - number // 4 - 1))
    mixed = jax.random.permutation(jax.random.fold_in(own, 3), amount)
    giver, sink = mixed[0:amount // 2 * 2:2], mixed[1:amount // 2 * 2:2]
    margin = jnp.minimum(tallies[giver] - 1, limit - tallies[sink]) // 2
    margin = jnp.where((giver == sequence[0]) | (sink == sequence[0]) | (tallies[sink] == 0), 0, jnp.maximum(margin, 0))
    moved = jax.random.randint(jax.random.fold_in(own, 4), (amount // 2,), 0, 1 << 20) % (margin + 1)
    tallies = tallies.at[giver].add(-moved).at[sink].add(moved)
    members = jnp.searchsorted(jnp.cumsum(tallies), jnp.arange(rows * top), side="right").astype(jnp.int32)
    table = members.reshape(top, rows).T
    table = table[jax.random.permutation(jax.random.fold_in(own, 1), rows)]
    rotation = jax.random.randint(jax.random.fold_in(own, 2), (rows, 1), 0, top)
    return jnp.take_along_axis(table, (jnp.arange(top)[None, :] + rotation) % top, axis=1)


def load_shares(number_of, total, most, slope, full):
    portions = [(1 << 20) // math.isqrt(grade ** slope) + 1 for grade in range(1, number_of + 1)]
    largest = most if full else min(most, max(-(-total // number_of), total * portions[0] // sum(portions)))
    least = 1 if total - largest >= number_of - 1 else 0
    counts, rest = [largest] + [least] * (number_of - 1), total - largest - least * (number_of - 1)
    while rest > 0:
        free = [i for i in range(1, number_of) if counts[i] < largest] or [i for i in range(1, number_of) if counts[i] < most]
        mass, left = sum([portions[i] for i in free]), rest
        for i in free:
            more = min(most - counts[i], max(1, left * portions[i] // mass), rest)
            counts[i] = counts[i] + more
            rest = rest - more
    return np.array(counts)


def gaussian(key, extent, deviation, reach, pieces=(), held_as=jnp.bfloat16):
    drawn = jax.random.normal(key, extent, jnp.float32) * deviation
    if len(pieces) > 0:
        drawn = level_of(key, extent, pieces, -0.22, 0.18) * drawn
    return jnp.clip(drawn, min=-reach, max=reach).astype(held_as)


def setup_inputs(seed: int = 0) -> dict:
    seeds = jax.random.split(jax.random.key(seed), 10)
    item_table = gaussian(seeds[0], (ITEMS, DE), 1.0, 6.0, ((0, 8),))
    cand_owner_keys = jax.random.split(jax.random.fold_in(seeds[1], 1), USERS * CAND // (CAND // N_CTX))
    cand_owner_turns = jax.random.permutation(jax.random.fold_in(seeds[1], 3), USERS * CAND // (CAND // N_CTX))
    cand_owner = jax.vmap(lambda own, number: routed_block(jax.random.fold_in(seeds[1], 2), own, number, CAND // N_CTX, N_REQ, 1, CAP, 2))(cand_owner_keys, cand_owner_turns).reshape((USERS, CAND, 1))
    cand_slot = set_ends(jax.random.randint(seeds[2], (USERS, CAND), 0, ITEMS_DEV), jax.random.fold_in(seeds[2], 1), 0, ITEMS_DEV - 1).astype(jnp.int32)
    w_in = gaussian(seeds[3], (DE, DM), DE ** -0.5, 0.375)
    w_uq = gaussian(seeds[4], (DM, 2 * DM), DM ** -0.5, 0.1875)
    w_out = gaussian(seeds[5], (DM, DM), DM ** -0.5, 0.1875)
    k_cache = gaussian(seeds[6], (USERS, HIST, DM), 2.0, 12.0, ((0, 8), (1, 4)))
    v_cache = gaussian(seeds[7], (USERS, HIST, DM), 1.0, 6.0, ((0, 8), (1, 4)))
    hist_len = draw_hist_len(jax.random.fold_in(seeds[9], 71), 0)
    return {"item_table": item_table, "cand_owner": cand_owner, "cand_slot": cand_slot, "w_in": w_in, "w_uq": w_uq, "w_out": w_out, "k_cache": k_cache, "v_cache": v_cache, "hist_len": hist_len}


def layer_norm(values):
    centre = lax.optimization_barrier(jnp.mean(values, axis=-1, keepdims=True))
    centred = values - centre
    spread = lax.optimization_barrier(jnp.mean(centred * centred, axis=-1, keepdims=True))
    return centred * lax.rsqrt(spread + 1e-05)

def attend_user(operands):
    query_rows, keys_user, values_user, length = operands
    block_size = math.gcd(HIST, 2048)
    block_count = HIST // block_size
    scale = DH ** (-0.5)
    query_heads = query_rows.reshape(CAND, HEADS, DH).astype(jnp.float32)

    def step(total, index):
        start = (index * block_size).astype(jnp.int32)
        key_block = lax.dynamic_slice_in_dim(keys_user, start, block_size, 0).reshape(block_size, HEADS, DH).astype(jnp.float32)
        value_block = lax.dynamic_slice_in_dim(values_user, start, block_size, 0).reshape(block_size, HEADS, DH).astype(jnp.float32)
        scores = jnp.einsum('qhd,khd->hqk', query_heads, key_block) * scale
        position = start + jnp.arange(block_size).astype(jnp.int32)
        weights = jnp.where(position[None, None, :] < length, jax.nn.silu(scores), 0.0)
        weights = lax.optimization_barrier(weights.astype(jnp.bfloat16)).astype(jnp.float32)
        added = jnp.einsum('hqk,khd->qhd', weights, value_block).reshape(CAND, DM)
        return (total + added, None)
    total, unused = lax.scan(step, jnp.zeros((CAND, DM), jnp.float32), jnp.arange(block_count).astype(jnp.int32))
    return total

def reference(item_table, cand_owner, cand_slot, w_in, w_uq, w_out, k_cache, v_cache, hist_len):
    table_rows = (cand_owner[:, :, 0] * ITEMS_DEV + cand_slot).astype(jnp.int32)
    embedded = item_table[table_rows].reshape(USERS * CAND, DE)
    features = jnp.dot(embedded, w_in, preferred_element_type=jnp.float32).astype(jnp.bfloat16)
    normed = layer_norm(features.astype(jnp.float32)).astype(jnp.bfloat16)
    projected = jax.nn.silu(jnp.dot(normed, w_uq, preferred_element_type=jnp.float32)).astype(jnp.bfloat16)
    gate_u = projected[:, :DM]
    query = projected[:, DM:].reshape(USERS, CAND, DM)
    attended = lax.map(attend_user, (query, k_cache, v_cache, hist_len)).reshape(USERS * CAND, DM)
    mixed = (layer_norm(attended) * gate_u.astype(jnp.float32)).astype(jnp.bfloat16)
    ranked = features.astype(jnp.float32) + jnp.dot(mixed, w_out, preferred_element_type=jnp.float32)
    return ranked.astype(jnp.bfloat16).reshape(USERS, CAND, DM)
```

```python
import functools

import jax
import jax.numpy as jnp
from jax import lax
from jax.experimental import pallas as pl
from jax.experimental.pallas import tpu as pltpu
from jax.sharding import PartitionSpec as P

HEADS = 8
KEY_BLOCK = 256
GROUP = 1024
VMEM = pl.BlockSpec(memory_space=pltpu.VMEM)
SMEM = pl.BlockSpec(memory_space=pltpu.SMEM)
F32 = jnp.float32
BF16 = jnp.bfloat16
NT = (((1,), (1,)), ((), ()))


def params(mib):
    return pltpu.CompilerParams(vmem_limit_bytes=mib << 20)


def layer_norm(values):
    centre = jnp.mean(values, axis=-1, keepdims=True)
    centred = values - centre
    spread = jnp.mean(centred * centred, axis=-1, keepdims=True)
    return centred * lax.rsqrt(spread + 1e-05)


def silu(values):
    half = values * 0.5
    return half + half * jnp.tanh(half)


def dot(a, b):
    return jnp.dot(a, b, preferred_element_type=F32)


def iota(shape, axis):
    return lax.broadcasted_iota(jnp.int32, shape, axis)


def hi_lo(row):
    wide = jnp.broadcast_to(row, (8, row.shape[1]))
    pick = iota(wide.shape, 0)
    parts = jnp.where(pick == 0, wide >> 8, jnp.where(pick == 1, wide & 255, 0))
    return parts.astype(F32).astype(BF16)


def ranks(owners, per):
    count = owners.shape[1]
    owner_count = lax.axis_size("req")
    codes = owners ^ lax.axis_index("req")
    named = iota((owner_count, count), 0) == codes
    row, column = iota((count, count), 0), iota((count, count), 1)
    earlier = ((row // per == column // per) & (row < column)).astype(F32).astype(BF16)
    before = dot(named.astype(F32).astype(BF16), earlier)
    rank = jnp.sum(jnp.where(named, before, 0.0), axis=0, keepdims=True)
    return codes, rank.astype(jnp.int32)


def code_of(peer, turn, peers):
    return turn * peers + (peer if turn % 2 == 0 else peers - 1 - peer)


def requests_kernel(per, cap, turns, owners_ref, slots_ref, *list_refs):
    peers = lax.axis_size("ctx")
    codes, rank = ranks(owners_ref[...], per)
    place = (iota(codes.shape, 1) // per) * cap + rank
    parts = hi_lo(slots_ref[...])
    length = peers * cap
    for turn in range(turns):
        code = code_of(lax.axis_index("ctx"), turn, peers)
        wanted = jnp.where(codes == code, place, -1)
        chosen = (iota((length, codes.shape[1]), 0) == wanted).astype(F32).astype(BF16)
        packed = lax.dot_general(parts, chosen, NT, preferred_element_type=F32)
        packed = packed[0:1] * 256.0 + packed[1:2]
        list_refs[turn][...] = packed.astype(jnp.int32)


def block_order(peers):
    return list(range(0, peers, 2)) + list(range(1, peers, 2))


def places_kernel(per, cap, turns, owners_ref, places_ref):
    peers = lax.axis_size("ctx")
    me = lax.axis_index("ctx")
    codes, rank = ranks(owners_ref[...], per)
    count = codes.shape[1]
    length = peers * cap
    turn = codes // peers
    inner = codes % peers
    peer = jnp.where(turn % 2 == 0, inner, peers - 1 - inner) ^ me
    buffer = jnp.zeros_like(peer)
    for bit, step in enumerate(exchange_steps(peers)):
        buffer = buffer + jnp.where((peer & step) != 0, 1 << bit, 0)
    place = (buffer * turns + turn) * length + (iota(codes.shape, 1) // per) * cap + rank
    row, column = iota((count, count), 0), iota((count, count), 1)
    block = row // per
    half = peers // 2
    relative = jnp.where(block < half, 2 * block, 2 * (block - half) + 1)
    source = (relative ^ me) * per + row % per
    order = (source == column).astype(F32).astype(BF16)
    found = lax.dot_general(order, hi_lo(place), NT, preferred_element_type=F32)
    found = (found[:, 0:1] * 256.0 + found[:, 1:2]).astype(jnp.int32)
    total = places_ref.shape[1]
    places_ref[...] = (iota((count, total), 1) == found).astype(F32).astype(BF16)


def exchange_steps(peers):
    steps, step = [], peers // 2
    while step >= 1:
        steps.append(step)
        step //= 2
    return steps


def lookup_kernel(list_ref, table_ref, rows_ref):
    length = list_ref.shape[1]
    same = (iota((length, length), 0) == iota((length, length), 1)).astype(F32).astype(BF16)
    found = lax.dot_general(same, hi_lo(list_ref[...]), NT, preferred_element_type=F32)
    found = (found[:, 0:1] * 256.0 + found[:, 1:2]).astype(jnp.int32)
    chosen = (iota((length, table_ref.shape[0]), 1) == found).astype(F32).astype(BF16)
    rows_ref[...] = dot(chosen, table_ref[...]).astype(BF16)


def project_kernel(per, buffers, *refs):
    places_ref, w_in_ref, w_uq_ref = refs[0], refs[1 + buffers], refs[2 + buffers]
    features_ref, gate_ref, query_ref = refs[3 + buffers :]
    width = w_in_ref.shape[1]
    embedded = None
    start = 0
    for received in refs[1 : 1 + buffers]:
        rows = received.shape[0]
        part = dot(places_ref[:, start : start + rows], received[...])
        embedded = part if embedded is None else embedded + part
        start += rows
    features = dot(embedded.astype(BF16), w_in_ref[...]).astype(BF16)
    features_ref[...] = features[:per]
    normed = layer_norm(features.astype(F32)).astype(BF16)
    query_ref[...] = silu(dot(normed, w_uq_ref[:, width:])).astype(BF16)
    gate_ref[...] = silu(dot(normed[:per], w_uq_ref[:, :width])).astype(BF16)


def attend_kernel(length_ref, query_ref, key_ref, value_ref, keep_ref, send_ref):
    events, head_dim = key_ref.shape
    scale = 0.5 * head_dim ** (-0.5)
    group = min(GROUP, events)
    block = min(KEY_BLOCK, group)
    valid = length_ref[0] - lax.axis_index("ctx") * events
    queries = query_ref[...]
    kept = keep_ref.shape[0]

    def add_group(first, total, masked):
        for inner in range(group // block):
            start = first + inner * block
            if not isinstance(start, int):
                start = pl.multiple_of(start, block)
            keys = key_ref[pl.ds(start, block), :]
            values = value_ref[pl.ds(start, block), :]
            if masked:
                inside = (iota((block, head_dim), 0) + start) < valid
                values = jnp.where(inside, values.astype(F32), 0.0).astype(BF16)
            half = lax.dot_general(queries, keys, NT, preferred_element_type=F32) * scale
            weights = (half + half * jnp.tanh(half)).astype(BF16)
            total = total + dot(weights, values)
        return total

    def store(total):
        keep_ref[...] = total[:kept]
        send_ref[...] = total[kept:].astype(BF16)

    zero = jnp.zeros((queries.shape[0], head_dim), F32)

    @pl.when(valid > events - group)
    def _():
        total = zero
        for first in range(0, events, group):
            total = add_group(first, total, first + group >= events)
        store(total)

    @pl.when(valid <= events - group)
    def _():
        trips = jnp.maximum(valid + group - 1, 0) // group
        store(lax.fori_loop(0, trips, lambda i, t: add_group(i * group, t, True), zero))


def finish_kernel(others, *refs):
    keep_ref, sibling_ref = refs[:2]
    gate_ref, features_ref, w_out_ref, out_ref = refs[2 + others :]
    attended = keep_ref[...] + sibling_ref[...].astype(F32)
    for other in refs[2 : 2 + others]:
        attended = attended + other[...].astype(F32)
    mixed = (layer_norm(attended) * gate_ref[...].astype(F32)).astype(BF16)
    ranked = features_ref[...].astype(F32) + dot(mixed, w_out_ref[...])
    out_ref[...] = ranked.astype(BF16)


def shards(item_table, cand_owner, cand_slot, w_in, w_uq, w_out, k_cache, v_cache, hist_len):
    users, peers = lax.axis_size("req"), lax.axis_size("ctx")
    count = cand_owner.shape[1]
    per = count // peers
    cap = max(2, 2 * per // users)
    turns = users // peers
    length = peers * cap
    width = w_out.shape[0]
    shape = jax.ShapeDtypeStruct

    def permute(values, target):
        pairs = []
        for user in range(users):
            for peer in range(peers):
                to_user, to_peer = target(user, peer)
                pairs.append((user * peers + peer, to_user * peers + to_peer))
        return lax.ppermute(values, ("req", "ctx"), pairs)

    def swap_owner(values, turn):
        return permute(values, lambda user, peer: (user ^ code_of(peer, turn, peers), peer))

    def swap_peer(values, step):
        return permute(values, lambda user, peer: (user, peer ^ step))

    owners = cand_owner.reshape(1, count)
    slots = cand_slot.reshape(1, count)
    lists = pl.pallas_call(
        functools.partial(requests_kernel, per, cap, turns),
        in_specs=[VMEM] * 2,
        out_specs=[VMEM] * turns,
        out_shape=[shape((1, length), jnp.int32)] * turns,
        compiler_params=params(16),
        name="requests",
    )(owners, slots)
    asked = [swap_owner(one, turn) for turn, one in enumerate(lists)]
    places = pl.pallas_call(
        functools.partial(places_kernel, per, cap, turns),
        in_specs=[VMEM],
        out_specs=VMEM,
        out_shape=shape((count, users * length), BF16),
        compiler_params=params(16),
        name="places",
    )(owners)
    rows = []
    for turn in range(turns):
        looked = pl.pallas_call(
            lookup_kernel,
            in_specs=[VMEM] * 2,
            out_specs=VMEM,
            out_shape=shape((length, item_table.shape[1]), BF16),
            compiler_params=params(16),
            name="lookup",
        )(asked[turn], item_table)
        rows.append(swap_owner(looked, turn))
    buffers = [jnp.concatenate(rows, axis=0)]
    for step in exchange_steps(peers):
        buffers = buffers + [swap_peer(one, step) for one in buffers]
    features, gate, queries = pl.pallas_call(
        functools.partial(project_kernel, per, len(buffers)),
        in_specs=[VMEM] * (3 + len(buffers)),
        out_specs=[VMEM] * 3,
        out_shape=[
            shape((per, width), BF16),
            shape((per, width), BF16),
            shape((count, width), BF16),
        ],
        compiler_params=params(32),
        name="project",
    )(places, *buffers, w_in, w_uq)
    keys, values = k_cache[0], v_cache[0]
    events = keys.shape[0]
    head_dim = width // HEADS
    half = count // 2
    keep, send = pl.pallas_call(
        attend_kernel,
        grid=(HEADS,),
        in_specs=[SMEM]
        + [pl.BlockSpec((rows_of, head_dim), lambda h: (0, h)) for rows_of in (count, events, events)],
        out_specs=[pl.BlockSpec((half, head_dim), lambda h: (0, h))] * 2,
        out_shape=[shape((half, width), F32), shape((half, width), BF16)],
        compiler_params=params(48),
        name="attend",
    )(hist_len, queries, keys, values)
    sibling = swap_peer(send, 1)
    others = []
    for index in range(1, peers // 2):
        piece = slice(index * per, (index + 1) * per)
        summed = (keep[piece] + sibling[piece].astype(F32)).astype(BF16)
        others.append(swap_peer(summed, 2 * index))
    ranked = pl.pallas_call(
        functools.partial(finish_kernel, len(others)),
        grid=(1,),
        in_specs=[pl.BlockSpec((per, width), lambda i: (0, 0))] * (4 + len(others))
        + [pl.BlockSpec((width, width), lambda i: (0, 0))],
        out_specs=pl.BlockSpec((per, width), lambda i: (0, 0)),
        out_shape=shape((per, width), BF16),
        compiler_params=params(24),
        name="finish",
    )(keep, sibling, *others, gate, features, w_out)
    return ranked[None]


def solution(mesh):
    in_specs = (
        P("req", None),
        P("req", None, None),
        P("req", None),
        P(),
        P(),
        P(),
        P("req", "ctx", None),
        P("req", "ctx", None),
        P("req"),
    )
    out_specs = P("req", "ctx", None)
    return jax.shard_map(shards, mesh=mesh, in_specs=in_specs, out_specs=out_specs, check_vma=False)
```

```python
import functools

import jax
import jax.numpy as jnp
from jax import lax
from jax.experimental import pallas as pl
from jax.experimental.pallas import tpu as pltpu
from jax.sharding import PartitionSpec as P

HEADS = 8
KEY_BLOCK = 256
GROUP = 1024
VMEM = pl.BlockSpec(memory_space=pltpu.VMEM)
HBM = pl.BlockSpec(memory_space=pltpu.HBM)
SMEM = pl.BlockSpec(memory_space=pltpu.SMEM)
F32 = jnp.float32
BF16 = jnp.bfloat16
NT = (((1,), (1,)), ((), ()))


def params(mib):
    return pltpu.CompilerParams(vmem_limit_bytes=mib << 20)


def layer_norm(values):
    centre = jnp.mean(values, axis=-1, keepdims=True)
    centred = values - centre
    spread = jnp.mean(centred * centred, axis=-1, keepdims=True)
    return centred * lax.rsqrt(spread + 1e-05)


def silu(values):
    half = values * 0.5
    return half + half * jnp.tanh(half)


def dot(a, b):
    return jnp.dot(a, b, preferred_element_type=F32)


def iota(shape, axis):
    return lax.broadcasted_iota(jnp.int32, shape, axis)


def hi_lo(row):
    wide = jnp.broadcast_to(row, (8, row.shape[1]))
    pick = iota(wide.shape, 0)
    parts = jnp.where(pick == 0, wide >> 8, jnp.where(pick == 1, wide & 255, 0))
    return parts.astype(F32).astype(BF16)


def ranks(packed, per):
    count = packed.shape[1]
    owner_count = lax.axis_size("req")
    codes = (packed >> 16) ^ lax.axis_index("req")
    named = iota((owner_count, count), 0) == codes
    row, column = iota((count, count), 0), iota((count, count), 1)
    earlier = ((row // per == column // per) & (row < column)).astype(F32).astype(BF16)
    before = dot(named.astype(F32).astype(BF16), earlier)
    rank = jnp.sum(jnp.where(named, before, 0.0), axis=0, keepdims=True)
    return codes, rank.astype(jnp.int32)


def code_of(peer, turn, peers):
    return turn * peers + (peer if turn % 2 == 0 else peers - 1 - peer)


def requests_kernel(per, cap, turns, packed_ref, *list_refs):
    peers = lax.axis_size("ctx")
    codes, rank = ranks(packed_ref[...], per)
    place = (iota(codes.shape, 1) // per) * cap + rank
    parts = hi_lo(packed_ref[...] & 65535)
    length = peers * cap
    for turn in range(turns):
        code = code_of(lax.axis_index("ctx"), turn, peers)
        wanted = jnp.where(codes == code, place, -1)
        chosen = (iota((length, codes.shape[1]), 0) == wanted).astype(F32).astype(BF16)
        packed = lax.dot_general(parts, chosen, NT, preferred_element_type=F32)
        packed = packed[0:1] * 256.0 + packed[1:2]
        list_refs[turn][...] = packed.astype(jnp.int32)


def places_kernel(per, cap, turns, packed_ref, places_ref, done_ref):
    peers = lax.axis_size("ctx")
    me = lax.axis_index("ctx")
    codes, rank = ranks(packed_ref[...], per)
    count = codes.shape[1]
    length = peers * cap
    turn = codes // peers
    inner = codes % peers
    peer = jnp.where(turn % 2 == 0, inner, peers - 1 - inner) ^ me
    buffer = jnp.zeros_like(peer)
    for bit, step in enumerate(exchange_steps(peers)):
        buffer = buffer + jnp.where((peer & step) != 0, 1 << bit, 0)
    place = (buffer * turns + turn) * length + (iota(codes.shape, 1) // per) * cap + rank
    row, column = iota((count, count), 0), iota((count, count), 1)
    block = row // per
    half = peers // 2
    relative = jnp.where(block < half, 2 * block, 2 * (block - half) + 1)
    source = (relative ^ me) * per + row % per
    order = (source == column).astype(F32).astype(BF16)
    found = lax.dot_general(order, hi_lo(place), NT, preferred_element_type=F32)
    found = (found[:, 0:1] * 256.0 + found[:, 1:2]).astype(jnp.int32)
    total = places_ref.shape[1]
    places_ref[...] = (iota((count, total), 1) == found).astype(F32).astype(BF16)
    done_ref[...] = jnp.zeros_like(done_ref)


def exchange_steps(peers):
    steps, step = [], peers // 2
    while step >= 1:
        steps.append(step)
        step //= 2
    return steps


def lookup_kernel(turns, table_ref, done_ref, *refs):
    del done_ref
    for list_ref, rows_ref in zip(refs[:turns], refs[turns:]):
        length = list_ref.shape[1]
        same = (iota((length, length), 0) == iota((length, length), 1)).astype(F32).astype(BF16)
        found = lax.dot_general(same, hi_lo(list_ref[...]), NT, preferred_element_type=F32)
        found = (found[:, 0:1] * 256.0 + found[:, 1:2]).astype(jnp.int32)
        chosen = (iota((length, table_ref.shape[0]), 1) == found).astype(F32).astype(BF16)
        rows_ref[...] = dot(chosen, table_ref[...]).astype(BF16)


def attend_kernel(per, buffers, length_ref, places_ref, *refs):
    received, refs = refs[:buffers], refs[buffers:]
    w_in_hbm, w_uq_hbm, keys_hbm, values_hbm = refs[:4]
    features_ref, normed_ref, keep_ref, send_ref = refs[4:8]
    queries_ref, keys_ref, values_ref, w_in_ref, w_query_ref, sems, weight_sems = refs[8:]
    heads, events, head_dim = keys_ref.shape
    width = heads * head_dim
    kept = keep_ref.shape[1]
    scale = 0.5 * head_dim ** (-0.5)
    group = min(GROUP, events)
    block = min(KEY_BLOCK, group)

    def copies(head):
        columns = pl.ds(pl.multiple_of(head * head_dim, head_dim), head_dim)
        return [
            pltpu.make_async_copy(hbm.at[:, columns], ref.at[head], sems.at[index, head])
            for index, (hbm, ref) in enumerate(((keys_hbm, keys_ref), (values_hbm, values_ref)))
        ]

    w_in_copy = pltpu.make_async_copy(w_in_hbm, w_in_ref, weight_sems.at[0])
    w_query_copy = pltpu.make_async_copy(
        w_uq_hbm.at[:, pl.ds(width, width)], w_query_ref, weight_sems.at[1]
    )
    w_in_copy.start()
    w_query_copy.start()

    @pl.loop(0, heads)
    def _(head):
        for copy in copies(head):
            copy.start()

    embedded = None
    start = 0
    for part_ref in received:
        rows = part_ref.shape[0]
        part = dot(places_ref[:, start : start + rows], part_ref[...])
        embedded = part if embedded is None else embedded + part
        start += rows
    w_in_copy.wait()
    features = dot(embedded.astype(BF16), w_in_ref[...]).astype(BF16)
    features_ref[...] = features[:per]
    normed = layer_norm(features.astype(F32)).astype(BF16)
    normed_ref[...] = normed[:per]
    w_query_copy.wait()
    for head in range(heads):
        columns = slice(head * head_dim, (head + 1) * head_dim)
        queries_ref[head] = silu(dot(normed, w_query_ref[:, columns])).astype(BF16)

    valid = length_ref[0] - lax.axis_index("ctx") * events

    def add_group(head, first, total, masked):
        for inner in range(group // block):
            start = first + inner * block
            if not isinstance(start, int):
                start = pl.multiple_of(start, block)
            keys = keys_ref[head, pl.ds(start, block), :]
            values = values_ref[head, pl.ds(start, block), :]
            if masked:
                inside = (iota((block, head_dim), 0) + start) < valid
                values = jnp.where(inside, values.astype(F32), 0.0).astype(BF16)
            half = lax.dot_general(queries_ref[head], keys, NT, preferred_element_type=F32) * scale
            weights = (half + half * jnp.tanh(half)).astype(BF16)
            total = total + dot(weights, values)
        return total

    def store(head, total):
        keep_ref[head] = total[:kept]
        send_ref[head] = total[kept:].astype(BF16)

    zero = jnp.zeros((queries_ref.shape[1], head_dim), F32)

    @pl.when(valid > events - group)
    def _():
        @pl.loop(0, heads)
        def _(head):
            for copy in copies(head):
                copy.wait()
            total = zero
            for first in range(0, events, group):
                total = add_group(head, first, total, first + group >= events)
            store(head, total)

    @pl.when(valid <= events - group)
    def _():
        trips = jnp.maximum(valid + group - 1, 0) // group

        @pl.loop(0, heads)
        def _(head):
            for copy in copies(head):
                copy.wait()
            store(
                head,
                lax.fori_loop(0, trips, lambda i, t: add_group(head, i * group, t, True), zero),
            )


def gate_kernel(normed_ref, w_uq_ref, gate_ref):
    gate_ref[...] = silu(dot(normed_ref[...], w_uq_ref[...])).astype(BF16)


def finish_kernel(others, *refs):
    keep_ref, sibling_ref = refs[:2]
    gate_ref, features_ref, w_out_ref, out_ref = refs[2 + others :]
    parts = []
    for head in range(keep_ref.shape[0]):
        part = keep_ref[head] + sibling_ref[head].astype(F32)
        for other in refs[2 : 2 + others]:
            part = part + other[head].astype(F32)
        parts.append(part)
    attended = jnp.concatenate(parts, axis=1)
    mixed = (layer_norm(attended) * gate_ref[...].astype(F32)).astype(BF16)
    ranked = features_ref[...].astype(F32) + dot(mixed, w_out_ref[...])
    out_ref[...] = ranked.astype(BF16)


def shards(item_table, cand_owner, cand_slot, w_in, w_uq, w_out, k_cache, v_cache, hist_len):
    users, peers = lax.axis_size("req"), lax.axis_size("ctx")
    count = cand_owner.shape[1]
    per = count // peers
    cap = max(2, 2 * per // users)
    turns = users // peers
    length = peers * cap
    width = w_out.shape[0]
    shape = jax.ShapeDtypeStruct

    def permute(values, target):
        pairs = []
        for user in range(users):
            for peer in range(peers):
                to_user, to_peer = target(user, peer)
                pairs.append((user * peers + peer, to_user * peers + to_peer))
        return lax.ppermute(values, ("req", "ctx"), pairs)

    def swap_owner(values, turn):
        return permute(values, lambda user, peer: (user ^ code_of(peer, turn, peers), peer))

    def swap_peer(values, step):
        return permute(values, lambda user, peer: (user, peer ^ step))

    packed = (cand_owner[:, :, 0] << 16) | cand_slot
    lists = pl.pallas_call(
        functools.partial(requests_kernel, per, cap, turns),
        in_specs=[VMEM],
        out_specs=[VMEM] * turns,
        out_shape=[shape((1, length), jnp.int32)] * turns,
        compiler_params=params(16),
        name="requests",
    )(packed)
    asked = [swap_owner(lists[turn], turn) for turn in reversed(range(turns))][::-1]
    places, places_done = pl.pallas_call(
        functools.partial(places_kernel, per, cap, turns),
        in_specs=[VMEM],
        out_specs=[VMEM] * 2,
        out_shape=[shape((count, users * length), BF16), shape((8, 128), jnp.int32)],
        compiler_params=params(16),
        cost_estimate=pl.CostEstimate(flops=1 << 28, bytes_accessed=24 << 20, transcendentals=0),
        name="places",
    )(packed)
    rows = pl.pallas_call(
        functools.partial(lookup_kernel, turns),
        in_specs=[VMEM] * (2 + turns),
        out_specs=[VMEM] * turns,
        out_shape=[shape((length, item_table.shape[1]), BF16)] * turns,
        compiler_params=params(16),
        name="lookup",
    )(item_table, places_done, *asked)
    rows = [swap_owner(rows[turn], turn) for turn in reversed(range(turns))][::-1]
    buffers = [jnp.concatenate(rows, axis=0)]
    for step in exchange_steps(peers):
        buffers = buffers + [swap_peer(one, step) for one in buffers]
    keys, values = k_cache[0], v_cache[0]
    events = keys.shape[0]
    head_dim = width // HEADS
    half = count // 2
    features, normed, keep, send = pl.pallas_call(
        functools.partial(attend_kernel, per, len(buffers)),
        in_specs=[SMEM] + [VMEM] * (1 + len(buffers)) + [HBM] * 4,
        out_specs=[VMEM] * 4,
        out_shape=[
            shape((per, width), BF16),
            shape((per, width), BF16),
            shape((HEADS, half, head_dim), F32),
            shape((HEADS, half, head_dim), BF16),
        ],
        scratch_shapes=[
            pltpu.VMEM((HEADS, count, head_dim), BF16),
            pltpu.VMEM((HEADS, events, head_dim), BF16),
            pltpu.VMEM((HEADS, events, head_dim), BF16),
            pltpu.VMEM(w_in.shape, BF16),
            pltpu.VMEM((width, width), BF16),
            pltpu.SemaphoreType.DMA((2, HEADS)),
            pltpu.SemaphoreType.DMA((2,)),
        ],
        compiler_params=params(47),
        name="attend",
    )(hist_len, places, *buffers, w_in, w_uq, keys, values)
    gate = pl.pallas_call(
        gate_kernel,
        grid=(1,),
        in_specs=[
            pl.BlockSpec((per, width), lambda i: (0, 0)),
            pl.BlockSpec((width, width), lambda i: (0, 0)),
        ],
        out_specs=pl.BlockSpec((per, width), lambda i: (0, 0)),
        out_shape=shape((per, width), BF16),
        compiler_params=params(16),
        cost_estimate=pl.CostEstimate(flops=1 << 28, bytes_accessed=3 << 20, transcendentals=0),
        name="gate",
    )(normed, w_uq)
    sibling = swap_peer(send, 1)
    others = []
    for index in range(1, peers // 2):
        piece = slice(index * per, (index + 1) * per)
        summed = (keep[:, piece] + sibling[:, piece].astype(F32)).astype(BF16)
        others.append(swap_peer(summed, 2 * index))
    block = pl.BlockSpec((HEADS, per, head_dim), lambda i: (0, 0, 0))
    ranked = pl.pallas_call(
        functools.partial(finish_kernel, len(others)),
        grid=(1,),
        in_specs=[block] * (2 + len(others))
        + [pl.BlockSpec((per, width), lambda i: (0, 0))] * 2
        + [pl.BlockSpec((width, width), lambda i: (0, 0))],
        out_specs=pl.BlockSpec((per, width), lambda i: (0, 0)),
        out_shape=shape((per, width), BF16),
        compiler_params=params(24),
        name="finish",
    )(keep, sibling, *others, gate, features, w_out)
    return ranked[None]


def solution(mesh):
    in_specs = (
        P("req", None),
        P("req", None, None),
        P("req", None),
        P(),
        P(),
        P(),
        P("req", "ctx", None),
        P("req", "ctx", None),
        P("req"),
    )
    out_specs = P("req", "ctx", None)
    return jax.shard_map(shards, mesh=mesh, in_specs=in_specs, out_specs=out_specs, check_vma=False)
```

```python
import functools

import jax
import jax.numpy as jnp
from jax import lax
from jax.experimental import pallas as pl
from jax.experimental.pallas import tpu as pltpu
from jax.sharding import PartitionSpec as P

HEADS = 8
KEY_BLOCK = 256
GROUP = 1024
VMEM = pl.BlockSpec(memory_space=pltpu.VMEM)
HBM = pl.BlockSpec(memory_space=pltpu.HBM)
SMEM = pl.BlockSpec(memory_space=pltpu.SMEM)
F32 = jnp.float32
BF16 = jnp.bfloat16
NT = (((1,), (1,)), ((), ()))


def params(mib):
    return pltpu.CompilerParams(vmem_limit_bytes=mib << 20)


def layer_norm(values):
    centre = jnp.mean(values, axis=-1, keepdims=True)
    centred = values - centre
    spread = jnp.mean(centred * centred, axis=-1, keepdims=True)
    return centred * lax.rsqrt(spread + 1e-05)


def silu(values):
    half = values * 0.5
    return half + half * jnp.tanh(half)


def dot(a, b):
    return jnp.dot(a, b, preferred_element_type=F32)


def iota(shape, axis):
    return lax.broadcasted_iota(jnp.int32, shape, axis)


def hi_lo(row):
    wide = jnp.broadcast_to(row, (8, row.shape[1]))
    pick = iota(wide.shape, 0)
    parts = jnp.where(pick == 0, wide >> 8, jnp.where(pick == 1, wide & 255, 0))
    return parts.astype(F32).astype(BF16)


def ranks(packed, per):
    count = packed.shape[1]
    owner_count = lax.axis_size("req")
    codes = (packed >> 16) ^ lax.axis_index("req") ^ (owner_count - 1)
    named = iota((owner_count, count), 0) == codes
    row, column = iota((count, count), 0), iota((count, count), 1)
    earlier = ((row // per == column // per) & (row < column)).astype(F32).astype(BF16)
    before = dot(named.astype(F32).astype(BF16), earlier)
    rank = jnp.sum(jnp.where(named, before, 0.0), axis=0, keepdims=True)
    return codes, rank.astype(jnp.int32)


def code_of(peer, turn, peers):
    return turn * peers + (peer if turn % 2 == 0 else peers - 1 - peer)


def requests_kernel(per, cap, turns, packed_ref, *list_refs):
    peers = lax.axis_size("ctx")
    codes, rank = ranks(packed_ref[...], per)
    place = (iota(codes.shape, 1) // per) * cap + rank
    parts = hi_lo(packed_ref[...] & 65535)
    length = peers * cap
    for turn in range(turns):
        code = code_of(lax.axis_index("ctx"), turn, peers)
        wanted = jnp.where(codes == code, place, -1)
        chosen = (iota((length, codes.shape[1]), 0) == wanted).astype(F32).astype(BF16)
        packed = lax.dot_general(parts, chosen, NT, preferred_element_type=F32)
        packed = packed[0:1] * 256.0 + packed[1:2]
        list_refs[turn][...] = packed.astype(jnp.int32)


def places_kernel(per, cap, turns, packed_ref, table_ref, w_in_ref, places_ref, *held):
    held[0][...] = table_ref[...]
    held[1][...] = w_in_ref[...]
    peers = lax.axis_size("ctx")
    me = lax.axis_index("ctx")
    codes, rank = ranks(packed_ref[...], per)
    count = codes.shape[1]
    length = peers * cap
    turn = codes // peers
    inner = codes % peers
    peer = jnp.where(turn % 2 == 0, inner, peers - 1 - inner) ^ me
    buffer = jnp.zeros_like(peer)
    for bit, step in enumerate(exchange_steps(peers)):
        buffer = buffer + jnp.where((peer & step) != 0, 1 << bit, 0)
    place = (buffer * turns + turn) * length + (iota(codes.shape, 1) // per) * cap + rank
    row, column = iota((count, count), 0), iota((count, count), 1)
    block = row // per
    half = peers // 2
    relative = jnp.where(block < half, 2 * block, 2 * (block - half) + 1)
    source = (relative ^ me) * per + row % per
    order = (source == column).astype(F32).astype(BF16)
    found = lax.dot_general(order, hi_lo(place), NT, preferred_element_type=F32)
    found = (found[:, 0:1] * 256.0 + found[:, 1:2]).astype(jnp.int32)
    total = places_ref.shape[1]
    places_ref[...] = (iota((count, total), 1) == found).astype(F32).astype(BF16)


def exchange_steps(peers):
    steps, step = [], peers // 2
    while step >= 1:
        steps.append(step)
        step //= 2
    return steps


def lookup_kernel(turns, table_ref, *refs):
    for list_ref, rows_ref in zip(refs[:turns], refs[turns:]):
        length = list_ref.shape[1]
        same = (iota((length, length), 0) == iota((length, length), 1)).astype(F32).astype(BF16)
        found = lax.dot_general(same, hi_lo(list_ref[...]), NT, preferred_element_type=F32)
        found = (found[:, 0:1] * 256.0 + found[:, 1:2]).astype(jnp.int32)
        chosen = (iota((length, table_ref.shape[0]), 1) == found).astype(F32).astype(BF16)
        rows_ref[...] = dot(chosen, table_ref[...]).astype(BF16)


def attend_kernel(per, buffers, length_ref, places_ref, *refs):
    received, refs = refs[:buffers], refs[buffers:]
    w_in_ref, w_uq_hbm, keys_hbm, values_hbm = refs[:4]
    features_ref, normed_ref, keep_ref, send_ref = refs[4:8]
    queries_ref, keys_ref, values_ref, w_query_ref, sems, weight_sem = refs[8:]
    heads, events, head_dim = keys_ref.shape
    width = heads * head_dim
    kept = keep_ref.shape[1]
    scale = 0.5 * head_dim ** (-0.5)
    group = min(GROUP, events)
    block = min(KEY_BLOCK, group)

    def copies(head):
        columns = pl.ds(pl.multiple_of(head * head_dim, head_dim), head_dim)
        return [
            pltpu.make_async_copy(hbm.at[:, columns], ref.at[head], sems.at[index, head])
            for index, (hbm, ref) in enumerate(((keys_hbm, keys_ref), (values_hbm, values_ref)))
        ]

    w_query_copy = pltpu.make_async_copy(
        w_uq_hbm.at[:, pl.ds(width, width)], w_query_ref, weight_sem
    )
    w_query_copy.start()

    @pl.loop(0, heads)
    def _(head):
        for copy in copies(head):
            copy.start()

    embedded = None
    start = 0
    for part_ref in received:
        rows = part_ref.shape[0]
        part = dot(places_ref[:, start : start + rows], part_ref[...])
        embedded = part if embedded is None else embedded + part
        start += rows
    features = dot(embedded.astype(BF16), w_in_ref[...]).astype(BF16)
    features_ref[...] = features[:per]
    normed = layer_norm(features.astype(F32)).astype(BF16)
    normed_ref[...] = normed[:per]
    w_query_copy.wait()
    together = 4
    for first in range(0, heads, together):
        columns = slice(first * head_dim, (first + together) * head_dim)
        queries = silu(dot(normed, w_query_ref[:, columns])).astype(BF16)
        for index in range(together):
            part = slice(index * head_dim, (index + 1) * head_dim)
            queries_ref[first + index] = queries[:, part]

    valid = length_ref[0] - lax.axis_index("ctx") * events

    def add_group(head, first, total, masked):
        def weights_of(start):
            keys = keys_ref[head, pl.ds(start, block), :]
            half = lax.dot_general(queries_ref[head], keys, NT, preferred_element_type=F32) * scale
            return (half + half * jnp.tanh(half)).astype(BF16)

        def values_of(start):
            values = values_ref[head, pl.ds(start, block), :]
            if masked:
                inside = (iota((block, head_dim), 0) + start) < valid
                values = jnp.where(inside, values.astype(F32), 0.0).astype(BF16)
            return values

        waiting = []
        for inner in range(group // block):
            start = first + inner * block
            if not isinstance(start, int):
                start = pl.multiple_of(start, block)
            waiting.append((weights_of(start), start))
            if len(waiting) > 0:
                weights, before = waiting.pop(0)
                total = total + dot(weights, values_of(before))
        for weights, before in waiting:
            total = total + dot(weights, values_of(before))
        return total

    def store(head, total):
        keep_ref[head] = total[:kept]
        send_ref[head] = total[kept:].astype(BF16)

    zero = jnp.zeros((queries_ref.shape[1], head_dim), F32)

    @pl.when(valid > events - group)
    def _():
        @pl.loop(0, heads // 4)
        def _(head):
            for one in [4 * head + extra for extra in range(4)]:
                for copy in copies(one):
                    copy.wait()
            for one in [4 * head + extra for extra in range(4)]:
                total = zero
                for first in range(0, events, group):
                    total = add_group(one, first, total, first + group >= events)
                store(one, total)

    @pl.when(valid <= events - group)
    def _():
        trips = jnp.maximum(valid + group - 1, 0) // group

        @pl.loop(0, heads)
        def _(head):
            for copy in copies(head):
                copy.wait()
            store(
                head,
                lax.fori_loop(0, trips, lambda i, t: add_group(head, i * group, t, True), zero),
            )


def gate_kernel(normed_ref, w_uq_ref, gate_ref):
    gate_ref[...] = silu(dot(normed_ref[...], w_uq_ref[...])).astype(BF16)


def finish_kernel(others, *refs):
    keep_ref, sibling_ref = refs[:2]
    gate_ref, features_ref, w_out_ref, out_ref = refs[2 + others :]
    parts = []
    for head in range(keep_ref.shape[0]):
        part = keep_ref[head] + sibling_ref[head].astype(F32)
        for other in refs[2 : 2 + others]:
            part = part + other[head].astype(F32)
        parts.append(part)
    attended = jnp.concatenate(parts, axis=1)
    mixed = (layer_norm(attended) * gate_ref[...].astype(F32)).astype(BF16)
    ranked = features_ref[...].astype(F32) + dot(mixed, w_out_ref[...])
    out_ref[...] = ranked.astype(BF16)


def shards(item_table, cand_owner, cand_slot, w_in, w_uq, w_out, k_cache, v_cache, hist_len):
    users, peers = lax.axis_size("req"), lax.axis_size("ctx")
    count = cand_owner.shape[1]
    per = count // peers
    cap = max(2, 2 * per // users)
    turns = users // peers
    length = peers * cap
    width = w_out.shape[0]
    shape = jax.ShapeDtypeStruct

    def permute(values, target):
        pairs = []
        for user in range(users):
            for peer in range(peers):
                to_user, to_peer = target(user, peer)
                pairs.append((user * peers + peer, to_user * peers + to_peer))
        return lax.ppermute(values, ("req", "ctx"), pairs)

    def swap_owner(values, turn):
        return permute(values, lambda user, peer: (user ^ (users - 1) ^ code_of(peer, turn, peers), peer))

    def swap_peer(values, step):
        return permute(values, lambda user, peer: (user, peer ^ step))

    packed = (cand_owner[:, :, 0] << 16) | cand_slot
    lists = pl.pallas_call(
        functools.partial(requests_kernel, per, cap, turns),
        in_specs=[VMEM],
        out_specs=[VMEM] * turns,
        out_shape=[shape((1, length), jnp.int32)] * turns,
        compiler_params=params(16),
        name="requests",
    )(packed)
    asked = [swap_owner(lists[turn], turn) for turn in reversed(range(turns))][::-1]
    places, table, w_in = pl.pallas_call(
        functools.partial(places_kernel, per, cap, turns),
        in_specs=[VMEM] * 3,
        out_specs=[VMEM] * 3,
        out_shape=[shape((count, users * length), BF16), shape(item_table.shape, BF16), shape(w_in.shape, BF16)],
        compiler_params=params(16),
        cost_estimate=pl.CostEstimate(flops=1 << 28, bytes_accessed=24 << 20, transcendentals=0),
        name="places",
    )(packed, item_table, w_in)
    rows = pl.pallas_call(
        functools.partial(lookup_kernel, turns),
        in_specs=[VMEM] * (1 + turns),
        out_specs=[VMEM] * turns,
        out_shape=[shape((length, item_table.shape[1]), BF16)] * turns,
        compiler_params=params(16),
        name="lookup",
    )(table, *asked)
    rows = [swap_owner(rows[turn], turn) for turn in reversed(range(turns))][::-1]
    buffers = [jnp.concatenate(rows, axis=0)]
    for step in exchange_steps(peers):
        buffers = buffers + [swap_peer(one, step) for one in buffers]
    keys, values = k_cache[0], v_cache[0]
    events = keys.shape[0]
    head_dim = width // HEADS
    half = count // 2
    features, normed, keep, send = pl.pallas_call(
        functools.partial(attend_kernel, per, len(buffers)),
        in_specs=[SMEM] + [VMEM] * (1 + len(buffers)) + [VMEM] + [HBM] * 3,
        out_specs=[VMEM] * 4,
        out_shape=[
            shape((per, width), BF16),
            shape((per, width), BF16),
            shape((HEADS, half, head_dim), F32),
            shape((HEADS, half, head_dim), BF16),
        ],
        scratch_shapes=[
            pltpu.VMEM((HEADS, count, head_dim), BF16),
            pltpu.VMEM((HEADS, events, head_dim), BF16),
            pltpu.VMEM((HEADS, events, head_dim), BF16),
            pltpu.VMEM((width, width), BF16),
            pltpu.SemaphoreType.DMA((2, HEADS)),
            pltpu.SemaphoreType.DMA,
        ],
        compiler_params=params(47),
        name="attend",
    )(hist_len, places, *buffers, w_in, w_uq, keys, values)
    gate = pl.pallas_call(
        gate_kernel,
        grid=(1,),
        in_specs=[
            pl.BlockSpec((per, width), lambda i: (0, 0)),
            pl.BlockSpec((width, width), lambda i: (0, 0)),
        ],
        out_specs=pl.BlockSpec((per, width), lambda i: (0, 0)),
        out_shape=shape((per, width), BF16),
        compiler_params=params(16),
        cost_estimate=pl.CostEstimate(flops=1 << 28, bytes_accessed=3 << 20, transcendentals=0),
        name="gate",
    )(normed, w_uq)
    sibling = swap_peer(send, 1)
    others = []
    for index in range(1, peers // 2):
        piece = slice(index * per, (index + 1) * per)
        summed = (keep[:, piece] + sibling[:, piece].astype(F32)).astype(BF16)
        others.append(swap_peer(summed, 2 * index))
    block = pl.BlockSpec((HEADS, per, head_dim), lambda i: (0, 0, 0))
    ranked = pl.pallas_call(
        functools.partial(finish_kernel, len(others)),
        grid=(1,),
        in_specs=[block] * (2 + len(others))
        + [pl.BlockSpec((per, width), lambda i: (0, 0))] * 2
        + [pl.BlockSpec((width, width), lambda i: (0, 0))],
        out_specs=pl.BlockSpec((per, width), lambda i: (0, 0)),
        out_shape=shape((per, width), BF16),
        compiler_params=params(24),
        name="finish",
    )(keep, sibling, *others, gate, features, w_out)
    return ranked[None]


def solution(mesh):
    in_specs = (
        P("req", None),
        P("req", None, None),
        P("req", None),
        P(),
        P(),
        P(),
        P("req", "ctx", None),
        P("req", "ctx", None),
        P("req"),
    )
    out_specs = P("req", "ctx", None)
    return jax.shard_map(shards, mesh=mesh, in_specs=in_specs, out_specs=out_specs, check_vma=False)
```

```python
import functools

import jax
import jax.numpy as jnp
from jax import lax
from jax.experimental import pallas as pl
from jax.experimental.pallas import tpu as pltpu
from jax.sharding import PartitionSpec as P

HEADS = 8
KEY_BLOCK = 256
GROUP = 1024
VMEM = pl.BlockSpec(memory_space=pltpu.VMEM)
HBM = pl.BlockSpec(memory_space=pltpu.HBM)
SMEM = pl.BlockSpec(memory_space=pltpu.SMEM)
F32 = jnp.float32
BF16 = jnp.bfloat16
NT = (((1,), (1,)), ((), ()))


def params(mib):
    return pltpu.CompilerParams(vmem_limit_bytes=mib << 20)


def layer_norm(values):
    centre = jnp.mean(values, axis=-1, keepdims=True)
    centred = values - centre
    spread = jnp.mean(centred * centred, axis=-1, keepdims=True)
    return centred * lax.rsqrt(spread + 1e-05)


def silu(values):
    half = values * 0.5
    return half + half * jnp.tanh(half)


def dot(a, b):
    return jnp.dot(a, b, preferred_element_type=F32)


def iota(shape, axis):
    return lax.broadcasted_iota(jnp.int32, shape, axis)


def hi_lo(row):
    wide = jnp.broadcast_to(row, (8, row.shape[1]))
    pick = iota(wide.shape, 0)
    parts = jnp.where(pick == 0, wide >> 8, jnp.where(pick == 1, wide & 255, 0))
    return parts.astype(F32).astype(BF16)


def ranks(packed, per):
    count = packed.shape[1]
    owner_count = lax.axis_size("req")
    codes = (packed >> 16) ^ lax.axis_index("req") ^ (owner_count - 1)
    named = iota((owner_count, count), 0) == codes
    row, column = iota((count, count), 0), iota((count, count), 1)
    earlier = ((row // per == column // per) & (row < column)).astype(F32).astype(BF16)
    before = dot(named.astype(F32).astype(BF16), earlier)
    rank = jnp.sum(jnp.where(named, before, 0.0), axis=0, keepdims=True)
    return codes, rank.astype(jnp.int32)


def code_of(peer, turn, peers):
    return turn * peers + (peer if turn % 2 == 0 else peers - 1 - peer)


def requests_kernel(per, cap, turns, packed_ref, *list_refs):
    peers = lax.axis_size("ctx")
    codes, rank = ranks(packed_ref[...], per)
    place = (iota(codes.shape, 1) // per) * cap + rank
    parts = hi_lo(packed_ref[...] & 65535)
    length = peers * cap
    for turn in range(turns):
        code = code_of(lax.axis_index("ctx"), turn, peers)
        wanted = jnp.where(codes == code, place, -1)
        chosen = (iota((length, codes.shape[1]), 0) == wanted).astype(F32).astype(BF16)
        packed = lax.dot_general(parts, chosen, NT, preferred_element_type=F32)
        packed = packed[0:1] * 256.0 + packed[1:2]
        list_refs[turn][...] = packed.astype(jnp.int32)


def hold_kernel(table_ref, held_ref):
    held_ref[...] = table_ref[...]


def places_kernel(per, cap, turns, packed_ref, rows_ref, w_in_ref, places_ref, held_ref):
    del rows_ref
    held_ref[...] = w_in_ref[...]
    peers = lax.axis_size("ctx")
    me = lax.axis_index("ctx")
    codes, rank = ranks(packed_ref[...], per)
    count = codes.shape[1]
    length = peers * cap
    turn = codes // peers
    inner = codes % peers
    peer = jnp.where(turn % 2 == 0, inner, peers - 1 - inner) ^ me
    buffer = jnp.zeros_like(peer)
    for bit, step in enumerate(exchange_steps(peers)):
        buffer = buffer + jnp.where((peer & step) != 0, 1 << bit, 0)
    place = (buffer * turns + turn) * length + (iota(codes.shape, 1) // per) * cap + rank
    row, column = iota((count, count), 0), iota((count, count), 1)
    block = row // per
    half = peers // 2
    relative = jnp.where(block < half, 2 * block, 2 * (block - half) + 1)
    source = (relative ^ me) * per + row % per
    order = (source == column).astype(F32).astype(BF16)
    found = lax.dot_general(order, hi_lo(place), NT, preferred_element_type=F32)
    found = (found[:, 0:1] * 256.0 + found[:, 1:2]).astype(jnp.int32)
    total = places_ref.shape[1]
    places_ref[...] = (iota((count, total), 1) == found).astype(F32).astype(BF16)


def exchange_steps(peers):
    steps, step = [], peers // 2
    while step >= 1:
        steps.append(step)
        step //= 2
    return steps


def lookup_kernel(turns, table_ref, *refs):
    refs[-1][...] = jnp.zeros_like(refs[-1])
    for list_ref, rows_ref in zip(refs[:turns], refs[turns:]):
        length = list_ref.shape[1]
        same = (iota((length, length), 0) == iota((length, length), 1)).astype(F32).astype(BF16)
        found = lax.dot_general(same, hi_lo(list_ref[...]), NT, preferred_element_type=F32)
        found = (found[:, 0:1] * 256.0 + found[:, 1:2]).astype(jnp.int32)
        chosen = (iota((length, table_ref.shape[0]), 1) == found).astype(F32).astype(BF16)
        rows_ref[...] = dot(chosen, table_ref[...]).astype(BF16)


def attend_kernel(per, buffers, length_ref, places_ref, *refs):
    received, refs = refs[:buffers], refs[buffers:]
    w_in_ref, w_uq_hbm, keys_hbm, values_hbm = refs[:4]
    features_ref, normed_ref, keep_ref, near_ref, far_ref = refs[4:9]
    queries_ref, keys_ref, values_ref, w_query_ref, sems, weight_sem = refs[9:]
    heads, events, head_dim = keys_ref.shape
    width = heads * head_dim
    kept = keep_ref.shape[1]
    scale = 0.5 * head_dim ** (-0.5)
    group = min(GROUP, events)
    block = min(KEY_BLOCK, group)

    def copies(head):
        columns = pl.ds(pl.multiple_of(head * head_dim, head_dim), head_dim)
        return [
            pltpu.make_async_copy(hbm.at[:, columns], ref.at[head], sems.at[index, head])
            for index, (hbm, ref) in enumerate(((keys_hbm, keys_ref), (values_hbm, values_ref)))
        ]

    w_query_copy = pltpu.make_async_copy(
        w_uq_hbm.at[:, pl.ds(width, width)], w_query_ref, weight_sem
    )
    w_query_copy.start()

    @pl.loop(0, heads)
    def _(head):
        for copy in copies(head):
            copy.start()

    embedded = None
    start = 0
    for part_ref in received:
        rows = part_ref.shape[0]
        part = dot(places_ref[:, start : start + rows], part_ref[...])
        embedded = part if embedded is None else embedded + part
        start += rows
    features = dot(embedded.astype(BF16), w_in_ref[...]).astype(BF16)
    features_ref[...] = features[:per]
    normed = layer_norm(features.astype(F32)).astype(BF16)
    normed_ref[...] = normed[:per]
    w_query_copy.wait()
    together = 4
    for first in range(0, heads, together):
        columns = slice(first * head_dim, (first + together) * head_dim)
        queries = silu(dot(normed, w_query_ref[:, columns])).astype(BF16)
        for index in range(together):
            part = slice(index * head_dim, (index + 1) * head_dim)
            queries_ref[first + index] = queries[:, part]

    valid = length_ref[0] - lax.axis_index("ctx") * events

    def add_group(head, first, total, masked):
        def weights_of(start):
            keys = keys_ref[head, pl.ds(start, block), :]
            half = lax.dot_general(queries_ref[head], keys, NT, preferred_element_type=F32) * scale
            return (half + half * jnp.tanh(half)).astype(BF16)

        def values_of(start):
            values = values_ref[head, pl.ds(start, block), :]
            if masked:
                inside = (iota((block, head_dim), 0) + start) < valid
                values = jnp.where(inside, values.astype(F32), 0.0).astype(BF16)
            return values

        waiting = []
        for inner in range(group // block):
            start = first + inner * block
            if not isinstance(start, int):
                start = pl.multiple_of(start, block)
            waiting.append((weights_of(start), start))
            if len(waiting) > 0:
                weights, before = waiting.pop(0)
                total = total + dot(weights, values_of(before))
        for weights, before in waiting:
            total = total + dot(weights, values_of(before))
        return total

    def store(head, total):
        keep_ref[head] = total[:kept]
        near_ref[head] = total[kept : kept + per].astype(BF16)
        far_ref[head] = total[kept + per :].astype(BF16)

    zero = jnp.zeros((queries_ref.shape[1], head_dim), F32)

    @pl.when(valid > events - group)
    def _():
        @pl.loop(0, heads // 4)
        def _(head):
            for extra in range(4):
                one = 4 * head + extra
                if extra % 2 == 0:
                    for copy in copies(one) + copies(one + 1):
                        copy.wait()
                total = zero
                for first in range(0, events, group):
                    total = add_group(one, first, total, first + group >= events)
                store(one, total)

    @pl.when(valid <= events - group)
    def _():
        trips = jnp.maximum(valid + group - 1, 0) // group

        @pl.loop(0, heads)
        def _(head):
            for copy in copies(head):
                copy.wait()
            store(
                head,
                lax.fori_loop(0, trips, lambda i, t: add_group(head, i * group, t, True), zero),
            )


def gate_kernel(normed_ref, w_uq_ref, gate_ref):
    gate_ref[...] = silu(dot(normed_ref[...], w_uq_ref[...])).astype(BF16)


def finish_kernel(others, *refs):
    keep_ref = refs[0]
    gate_ref, features_ref, w_out_ref, out_ref = refs[1 + others :]
    parts = []
    for head in range(keep_ref.shape[0]):
        part = keep_ref[head]
        for other in refs[1 : 1 + others]:
            part = part + other[head].astype(F32)
        parts.append(part)
    attended = jnp.concatenate(parts, axis=1)
    mixed = (layer_norm(attended) * gate_ref[...].astype(F32)).astype(BF16)
    ranked = features_ref[...].astype(F32) + dot(mixed, w_out_ref[...])
    out_ref[...] = ranked.astype(BF16)


def shards(item_table, cand_owner, cand_slot, w_in, w_uq, w_out, k_cache, v_cache, hist_len):
    users, peers = lax.axis_size("req"), lax.axis_size("ctx")
    count = cand_owner.shape[1]
    per = count // peers
    cap = max(2, 2 * per // users)
    turns = users // peers
    length = peers * cap
    width = w_out.shape[0]
    shape = jax.ShapeDtypeStruct

    def permute(values, target):
        pairs = []
        for user in range(users):
            for peer in range(peers):
                to_user, to_peer = target(user, peer)
                pairs.append((user * peers + peer, to_user * peers + to_peer))
        return lax.ppermute(values, ("req", "ctx"), pairs)

    def swap_owner(values, turn):
        return permute(values, lambda user, peer: (user ^ (users - 1) ^ code_of(peer, turn, peers), peer))

    def swap_peer(values, step):
        return permute(values, lambda user, peer: (user, peer ^ step))

    packed = (cand_owner[:, :, 0] << 16) | cand_slot
    lists = pl.pallas_call(
        functools.partial(requests_kernel, per, cap, turns),
        in_specs=[VMEM],
        out_specs=[VMEM] * turns,
        out_shape=[shape((1, length), jnp.int32)] * turns,
        compiler_params=params(16),
        name="requests",
    )(packed)
    asked = [swap_owner(lists[turn], turn) for turn in reversed(range(turns))][::-1]
    table = pl.pallas_call(
        hold_kernel,
        in_specs=[VMEM],
        out_specs=VMEM,
        out_shape=shape(item_table.shape, BF16),
        compiler_params=params(16),
        cost_estimate=pl.CostEstimate(flops=1 << 20, bytes_accessed=24 << 20, transcendentals=0),
        name="hold",
    )(item_table)
    looked = pl.pallas_call(
        functools.partial(lookup_kernel, turns),
        in_specs=[VMEM] * (1 + turns),
        out_specs=[VMEM] * (turns + 1),
        out_shape=[shape((length, item_table.shape[1]), BF16)] * turns
        + [shape((8, 128), BF16)],
        compiler_params=params(16),
        name="lookup",
    )(table, *asked)
    places, w_in = pl.pallas_call(
        functools.partial(places_kernel, per, cap, turns),
        in_specs=[VMEM] * 3,
        out_specs=[VMEM] * 2,
        out_shape=[shape((count, users * length), BF16), shape(w_in.shape, BF16)],
        compiler_params=params(16),
        cost_estimate=pl.CostEstimate(flops=1 << 28, bytes_accessed=24 << 20, transcendentals=0),
        name="places",
    )(packed, looked[-1], w_in)
    rows = [swap_owner(looked[turn], turn) for turn in reversed(range(turns))][::-1]
    *rows, places, w_in = lax.optimization_barrier((*rows, places, w_in))
    buffers = [jnp.concatenate(rows, axis=0)]
    for step in exchange_steps(peers):
        buffers = buffers + [swap_peer(one, step) for one in buffers]
    keys, values = k_cache[0], v_cache[0]
    events = keys.shape[0]
    head_dim = width // HEADS
    half = count // 2
    features, normed, keep, near, far = pl.pallas_call(
        functools.partial(attend_kernel, per, len(buffers)),
        in_specs=[SMEM] + [VMEM] * (1 + len(buffers)) + [VMEM] + [HBM] * 3,
        out_specs=[VMEM] * 5,
        out_shape=[
            shape((per, width), BF16),
            shape((per, width), BF16),
            shape((HEADS, half, head_dim), F32),
            shape((HEADS, per, head_dim), BF16),
            shape((HEADS, half - per, head_dim), BF16),
        ],
        scratch_shapes=[
            pltpu.VMEM((HEADS, count, head_dim), BF16),
            pltpu.VMEM((HEADS, events, head_dim), BF16),
            pltpu.VMEM((HEADS, events, head_dim), BF16),
            pltpu.VMEM((width, width), BF16),
            pltpu.SemaphoreType.DMA((2, HEADS)),
            pltpu.SemaphoreType.DMA,
        ],
        compiler_params=params(47),
        name="attend",
    )(hist_len, places, *buffers, w_in, w_uq, keys, values)
    gate = pl.pallas_call(
        gate_kernel,
        grid=(1,),
        in_specs=[
            pl.BlockSpec((per, width), lambda i: (0, 0)),
            pl.BlockSpec((width, width), lambda i: (0, 0)),
        ],
        out_specs=pl.BlockSpec((per, width), lambda i: (0, 0)),
        out_shape=shape((per, width), BF16),
        compiler_params=params(16),
        cost_estimate=pl.CostEstimate(flops=1 << 28, bytes_accessed=3 << 20, transcendentals=0),
        name="gate",
    )(normed, w_uq)
    sibling = swap_peer(far, 1)
    sums = []
    for index in range(1, peers // 2):
        piece = slice((index - 1) * per, index * per)
        kept = keep[:, index * per : (index + 1) * per]
        sums.append((kept + sibling[:, piece].astype(F32)).astype(BF16))
    near, *sums = lax.optimization_barrier((near, *sums))
    others = [swap_peer(one, 2 * index) for index, one in enumerate(sums, 1)]
    others.append(swap_peer(near, 1))
    block = pl.BlockSpec((HEADS, per, head_dim), lambda i: (0, 0, 0))
    ranked = pl.pallas_call(
        functools.partial(finish_kernel, len(others)),
        grid=(1,),
        in_specs=[block] * (1 + len(others))
        + [pl.BlockSpec((per, width), lambda i: (0, 0))] * 2
        + [pl.BlockSpec((width, width), lambda i: (0, 0))],
        out_specs=pl.BlockSpec((per, width), lambda i: (0, 0)),
        out_shape=shape((per, width), BF16),
        compiler_params=params(24),
        name="finish",
    )(keep, *others, gate, features, w_out)
    return ranked[None]


def solution(mesh):
    in_specs = (
        P("req", None),
        P("req", None, None),
        P("req", None),
        P(),
        P(),
        P(),
        P("req", "ctx", None),
        P("req", "ctx", None),
        P("req"),
    )
    out_specs = P("req", "ctx", None)
    return jax.shard_map(shards, mesh=mesh, in_specs=in_specs, out_specs=out_specs, check_vma=False)
```

```python
import functools

import jax
import jax.numpy as jnp
from jax import lax
from jax.experimental import pallas as pl
from jax.experimental.pallas import tpu as pltpu
from jax.sharding import PartitionSpec as P

HEADS = 8
CORES = 2
KEY_BLOCK = 256
GROUP = 1024
VMEM = pl.BlockSpec(memory_space=pltpu.VMEM)
HBM = pl.BlockSpec(memory_space=pltpu.HBM)
SMEM = pl.BlockSpec(memory_space=pltpu.SMEM)
F32 = jnp.float32
BF16 = jnp.bfloat16
NT = (((1,), (1,)), ((), ()))


def params(mib):
    return pltpu.CompilerParams(vmem_limit_bytes=mib << 20)


def layer_norm(values):
    centre = jnp.mean(values, axis=-1, keepdims=True)
    centred = values - centre
    spread = jnp.mean(centred * centred, axis=-1, keepdims=True)
    return centred * lax.rsqrt(spread + 1e-05)


def silu(values):
    half = values * 0.5
    return half + half * jnp.tanh(half)


def dot(a, b):
    return jnp.dot(a, b, preferred_element_type=F32)


def iota(shape, axis):
    return lax.broadcasted_iota(jnp.int32, shape, axis)


def hi_lo(row):
    wide = jnp.broadcast_to(row, (8, row.shape[1]))
    pick = iota(wide.shape, 0)
    parts = jnp.where(pick == 0, wide >> 8, jnp.where(pick == 1, wide & 255, 0))
    return parts.astype(F32).astype(BF16)


def ranks(packed, per):
    count = packed.shape[1]
    owner_count = lax.axis_size("req")
    codes = (packed >> 16) ^ lax.axis_index("req") ^ (owner_count - 1)
    named = iota((owner_count, count), 0) == codes
    row, column = iota((count, count), 0), iota((count, count), 1)
    earlier = ((row // per == column // per) & (row < column)).astype(F32).astype(BF16)
    before = dot(named.astype(F32).astype(BF16), earlier)
    rank = jnp.sum(jnp.where(named, before, 0.0), axis=0, keepdims=True)
    return codes, rank.astype(jnp.int32)


def code_of(core, turn):
    return turn * CORES + (core if turn % 2 == 0 else CORES - 1 - core)


def requests_kernel(per, cap, turns, packed_ref, *list_refs):
    peers = lax.axis_size("ctx")
    codes, rank = ranks(packed_ref[...], per)
    place = (iota(codes.shape, 1) // per) * cap + rank
    parts = hi_lo(packed_ref[...] & 65535)
    length = peers * cap
    for turn in range(turns):
        code = code_of(lax.axis_index("ctx") % CORES, turn)
        wanted = jnp.where(codes == code, place, -1)
        chosen = (iota((length, codes.shape[1]), 0) == wanted).astype(F32).astype(BF16)
        packed = lax.dot_general(parts, chosen, NT, preferred_element_type=F32)
        packed = packed[0:1] * 256.0 + packed[1:2]
        list_refs[turn][...] = packed.astype(jnp.int32)


def hold_kernel(table_ref, held_ref, done_ref):
    done_ref[...] = jnp.zeros_like(done_ref)
    held_ref[...] = table_ref[...]


def places_kernel(per, cap, turns, packed_ref, rows_ref, w_in_ref, places_ref, held_ref):
    del rows_ref
    held_ref[...] = w_in_ref[...]
    peers = lax.axis_size("ctx")
    me = lax.axis_index("ctx")
    codes, rank = ranks(packed_ref[...], per)
    count = codes.shape[1]
    length = peers * cap
    turn = codes // CORES
    inner = codes % CORES
    core = jnp.where(turn % 2 == 0, inner, CORES - 1 - inner)
    buffer = jnp.where(core == me % CORES, 0, 1)
    place = (buffer * turns + turn) * length + (iota(codes.shape, 1) // per) * cap + rank
    row, column = iota((count, count), 0), iota((count, count), 1)
    block = row // per
    half = peers // 2
    relative = jnp.where(block < half, 2 * block, 2 * (block - half) + 1)
    source = (relative ^ me) * per + row % per
    order = (source == column).astype(F32).astype(BF16)
    found = lax.dot_general(order, hi_lo(place), NT, preferred_element_type=F32)
    found = (found[:, 0:1] * 256.0 + found[:, 1:2]).astype(jnp.int32)
    total = places_ref.shape[1]
    places_ref[...] = (iota((count, total), 1) == found).astype(F32).astype(BF16)


def lookup_kernel(turns, table_ref, done_ref, *refs):
    del done_ref
    refs[-1][...] = jnp.zeros_like(refs[-1])
    for list_ref, rows_ref in zip(refs[:turns], refs[turns:]):
        length = list_ref.shape[1]
        same = (iota((length, length), 0) == iota((length, length), 1)).astype(F32).astype(BF16)
        found = lax.dot_general(same, hi_lo(list_ref[...]), NT, preferred_element_type=F32)
        high, low = found[:, 0:1].astype(jnp.int32), found[:, 1:2].astype(jnp.int32)
        parts = table_ref.shape[0] // 256
        same_low = iota((length, 256), 1) == low
        chosen = [
            jnp.where(same_low & (high == part), 1.0, 0.0).astype(BF16) for part in range(parts)
        ]
        rows_ref[...] = dot(jnp.concatenate(chosen, axis=1), table_ref[...]).astype(BF16)


def attend_kernel(per, buffers, length_ref, places_ref, *refs):
    received, refs = refs[:buffers], refs[buffers:]
    w_in_ref, w_uq_hbm, keys_hbm, values_hbm = refs[:4]
    features_ref, normed_ref, keep_ref, near_ref, far_ref = refs[4:9]
    queries_ref, keys_ref, values_ref, w_query_ref, sems, weight_sem = refs[9:]
    heads, events, head_dim = keys_ref.shape
    width = heads * head_dim
    kept = keep_ref.shape[1]
    scale = 0.5 * head_dim ** (-0.5)
    group = min(GROUP, events)
    block = min(KEY_BLOCK, group)

    def copies(head):
        columns = pl.ds(pl.multiple_of(head * head_dim, head_dim), head_dim)
        return [
            pltpu.make_async_copy(hbm.at[:, columns], ref.at[head], sems.at[index, head])
            for index, (hbm, ref) in enumerate(((keys_hbm, keys_ref), (values_hbm, values_ref)))
        ]

    w_query_copy = pltpu.make_async_copy(
        w_uq_hbm.at[:, pl.ds(width, width)], w_query_ref, weight_sem
    )
    w_query_copy.start()

    @pl.loop(0, heads)
    def _(head):
        for copy in copies(head):
            copy.start()

    embedded = None
    start = 0
    for part_ref in received:
        rows = part_ref.shape[0]
        part = dot(places_ref[:, start : start + rows], part_ref[...])
        embedded = part if embedded is None else embedded + part
        start += rows
    features = dot(embedded.astype(BF16), w_in_ref[...]).astype(BF16)
    features_ref[...] = features[:per]
    normed = layer_norm(features.astype(F32)).astype(BF16)
    normed_ref[...] = normed[:per]
    w_query_copy.wait()
    together = 4
    for first in range(0, heads, together):
        columns = slice(first * head_dim, (first + together) * head_dim)
        queries = silu(dot(normed, w_query_ref[:, columns])).astype(BF16)
        for index in range(together):
            part = slice(index * head_dim, (index + 1) * head_dim)
            queries_ref[first + index] = queries[:, part]

    valid = length_ref[0] - lax.axis_index("ctx") * events

    def add_group(head, first, total, masked):
        def weights_of(start):
            keys = keys_ref[head, pl.ds(start, block), :]
            half = lax.dot_general(queries_ref[head], keys, NT, preferred_element_type=F32) * scale
            return (half + half * jnp.tanh(half)).astype(BF16)

        def values_of(start):
            values = values_ref[head, pl.ds(start, block), :]
            if masked:
                inside = (iota((block, head_dim), 0) + start) < valid
                values = jnp.where(inside, values.astype(F32), 0.0).astype(BF16)
            return values

        waiting = []
        for inner in range(group // block):
            start = first + inner * block
            if not isinstance(start, int):
                start = pl.multiple_of(start, block)
            waiting.append((weights_of(start), start))
            if len(waiting) > 0:
                weights, before = waiting.pop(0)
                total = total + dot(weights, values_of(before))
        for weights, before in waiting:
            total = total + dot(weights, values_of(before))
        return total

    def store(head, total):
        keep_ref[head] = total[:kept]
        near_ref[head] = total[kept : kept + per].astype(BF16)
        far_ref[head] = total[kept + per :].astype(BF16)

    zero = jnp.zeros((queries_ref.shape[1], head_dim), F32)

    @pl.when(valid > events - group)
    def _():
        @pl.loop(0, heads // 4)
        def _(head):
            for extra in range(4):
                one = 4 * head + extra
                if extra % 2 == 0:
                    for copy in copies(one) + copies(one + 1):
                        copy.wait()
                total = zero
                for first in range(0, events, group):
                    total = add_group(one, first, total, first + group >= events)
                store(one, total)

    @pl.when(valid <= events - group)
    def _():
        trips = jnp.maximum(valid + group - 1, 0) // group

        @pl.loop(0, heads)
        def _(head):
            for copy in copies(head):
                copy.wait()
            store(
                head,
                lax.fori_loop(0, trips, lambda i, t: add_group(head, i * group, t, True), zero),
            )


def gate_kernel(normed_ref, w_uq_ref, gate_ref):
    gate_ref[...] = silu(dot(normed_ref[...], w_uq_ref[...])).astype(BF16)


def finish_kernel(others, *refs):
    keep_ref = refs[0]
    gate_ref, features_ref, w_out_ref, out_ref = refs[1 + others :]
    parts = []
    for head in range(keep_ref.shape[0]):
        part = keep_ref[head]
        for other in refs[1 : 1 + others]:
            part = part + other[head].astype(F32)
        parts.append(part)
    attended = jnp.concatenate(parts, axis=1)
    mixed = (layer_norm(attended) * gate_ref[...].astype(F32)).astype(BF16)
    ranked = features_ref[...].astype(F32) + dot(mixed, w_out_ref[...])
    out_ref[...] = ranked.astype(BF16)


def shards(item_table, cand_owner, cand_slot, w_in, w_uq, w_out, k_cache, v_cache, hist_len):
    users, peers = lax.axis_size("req"), lax.axis_size("ctx")
    count = cand_owner.shape[1]
    per = count // peers
    cap = max(2, 2 * per // users)
    turns = users // CORES
    length = peers * cap
    width = w_out.shape[0]
    shape = jax.ShapeDtypeStruct

    def permute(values, target):
        pairs = []
        for user in range(users):
            for peer in range(peers):
                to_user, to_peer = target(user, peer)
                pairs.append((user * peers + peer, to_user * peers + to_peer))
        return lax.ppermute(values, ("req", "ctx"), pairs)

    def swap_owner(values, turn):
        return permute(values, lambda user, peer: (user ^ (users - 1) ^ code_of(peer % CORES, turn), peer))

    def swap_peer(values, step):
        return permute(values, lambda user, peer: (user, peer ^ step))

    packed = (cand_owner[:, :, 0] << 16) | cand_slot
    lists = pl.pallas_call(
        functools.partial(requests_kernel, per, cap, turns),
        in_specs=[VMEM],
        out_specs=[VMEM] * turns,
        out_shape=[shape((1, length), jnp.int32)] * turns,
        compiler_params=params(16),
        name="requests",
    )(packed)
    asked = [swap_owner(lists[turn], turn) for turn in reversed(range(turns))][::-1]
    table, table_done = pl.pallas_call(
        hold_kernel,
        in_specs=[VMEM],
        out_specs=[VMEM] * 2,
        out_shape=[shape(item_table.shape, BF16), shape((8, 128), BF16)],
        compiler_params=params(16),
        cost_estimate=pl.CostEstimate(flops=1 << 20, bytes_accessed=24 << 20, transcendentals=0),
        name="hold",
    )(item_table)
    looked, looked_done = [], table_done
    for group in (asked[: turns // 2], asked[turns // 2 :]):
        *found, looked_done = pl.pallas_call(
            functools.partial(lookup_kernel, len(group)),
            in_specs=[VMEM] * (2 + len(group)),
            out_specs=[VMEM] * (len(group) + 1),
            out_shape=[shape((length, item_table.shape[1]), BF16)] * len(group)
            + [shape((8, 128), BF16)],
            compiler_params=params(16),
            name="lookup",
        )(table, looked_done, *group)
        looked = looked + found
    places, w_in = pl.pallas_call(
        functools.partial(places_kernel, per, cap, turns),
        in_specs=[VMEM] * 3,
        out_specs=[VMEM] * 2,
        out_shape=[shape((count, users * length), BF16), shape(w_in.shape, BF16)],
        compiler_params=params(16),
        cost_estimate=pl.CostEstimate(flops=1 << 28, bytes_accessed=24 << 20, transcendentals=0),
        name="places",
    )(packed, looked_done, w_in)
    rows = [swap_owner(looked[turn], turn) for turn in reversed(range(turns))][::-1]
    *rows, places, w_in = lax.optimization_barrier((*rows, places, w_in))
    fetched = jnp.concatenate(rows, axis=0)
    buffers = [fetched, swap_peer(fetched, 1)]
    keys, values = k_cache[0], v_cache[0]
    events = keys.shape[0]
    head_dim = width // HEADS
    half = count // 2
    features, normed, keep, near, far = pl.pallas_call(
        functools.partial(attend_kernel, per, len(buffers)),
        in_specs=[SMEM] + [VMEM] * (1 + len(buffers)) + [VMEM] + [HBM] * 3,
        out_specs=[VMEM] * 5,
        out_shape=[
            shape((per, width), BF16),
            shape((per, width), BF16),
            shape((HEADS, half, head_dim), F32),
            shape((HEADS, per, head_dim), BF16),
            shape((HEADS, half - per, head_dim), BF16),
        ],
        scratch_shapes=[
            pltpu.VMEM((HEADS, count, head_dim), BF16),
            pltpu.VMEM((HEADS, events, head_dim), BF16),
            pltpu.VMEM((HEADS, events, head_dim), BF16),
            pltpu.VMEM((width, width), BF16),
            pltpu.SemaphoreType.DMA((2, HEADS)),
            pltpu.SemaphoreType.DMA,
        ],
        compiler_params=params(47),
        name="attend",
    )(hist_len, places, *buffers, w_in, w_uq, keys, values)
    gate = pl.pallas_call(
        gate_kernel,
        grid=(1,),
        in_specs=[
            pl.BlockSpec((per, width), lambda i: (0, 0)),
            pl.BlockSpec((width, width), lambda i: (0, 0)),
        ],
        out_specs=pl.BlockSpec((per, width), lambda i: (0, 0)),
        out_shape=shape((per, width), BF16),
        compiler_params=params(16),
        cost_estimate=pl.CostEstimate(flops=1 << 28, bytes_accessed=3 << 20, transcendentals=0),
        name="gate",
    )(normed, w_uq)
    sibling = swap_peer(far, 1)
    sums = []
    for index in range(1, peers // 2):
        piece = slice((index - 1) * per, index * per)
        kept = keep[:, index * per : (index + 1) * per]
        sums.append((kept + sibling[:, piece].astype(F32)).astype(BF16))
    near, *sums = lax.optimization_barrier((near, *sums))
    others = [swap_peer(one, 2 * index) for index, one in enumerate(sums, 1)]
    others.append(swap_peer(near, 1))
    block = pl.BlockSpec((HEADS, per, head_dim), lambda i: (0, 0, 0))
    ranked = pl.pallas_call(
        functools.partial(finish_kernel, len(others)),
        grid=(1,),
        in_specs=[block] * (1 + len(others))
        + [pl.BlockSpec((per, width), lambda i: (0, 0))] * 2
        + [pl.BlockSpec((width, width), lambda i: (0, 0))],
        out_specs=pl.BlockSpec((per, width), lambda i: (0, 0)),
        out_shape=shape((per, width), BF16),
        compiler_params=params(24),
        name="finish",
    )(keep, *others, gate, features, w_out)
    return ranked[None]


def solution(mesh):
    in_specs = (
        P("req", None),
        P("req", None, None),
        P("req", None),
        P(),
        P(),
        P(),
        P("req", "ctx", None),
        P("req", "ctx", None),
        P("req"),
    )
    out_specs = P("req", "ctx", None)
    return jax.shard_map(shards, mesh=mesh, in_specs=in_specs, out_specs=out_specs, check_vma=False)
```

```python
import functools

import jax
import jax.numpy as jnp
from jax import lax
from jax.experimental import pallas as pl
from jax.experimental.pallas import tpu as pltpu
from jax.sharding import PartitionSpec as P

HEADS = 8
CORES = 2
KEY_BLOCK = 256
GROUP = 1024
VMEM = pl.BlockSpec(memory_space=pltpu.VMEM)
HBM = pl.BlockSpec(memory_space=pltpu.HBM)
SMEM = pl.BlockSpec(memory_space=pltpu.SMEM)
F32 = jnp.float32
BF16 = jnp.bfloat16
NT = (((1,), (1,)), ((), ()))


def params(mib):
    return pltpu.CompilerParams(vmem_limit_bytes=mib << 20)


def layer_norm(values):
    centre = jnp.mean(values, axis=-1, keepdims=True)
    centred = values - centre
    spread = jnp.mean(centred * centred, axis=-1, keepdims=True)
    return centred * lax.rsqrt(spread + 1e-05)


def silu(values):
    half = values * 0.5
    return half + half * jnp.tanh(half)


def dot(a, b):
    return jnp.dot(a, b, preferred_element_type=F32)


def iota(shape, axis):
    return lax.broadcasted_iota(jnp.int32, shape, axis)


def hi_lo(row):
    wide = jnp.broadcast_to(row, (8, row.shape[1]))
    pick = iota(wide.shape, 0)
    parts = jnp.where(pick == 0, wide >> 8, jnp.where(pick == 1, wide & 255, 0))
    return parts.astype(F32).astype(BF16)


def ranks(packed, per):
    count = packed.shape[1]
    owner_count = lax.axis_size("req")
    codes = (packed >> 16) ^ lax.axis_index("req") ^ (owner_count - 1)
    named = iota((owner_count, count), 0) == codes
    row, column = iota((count, count), 0), iota((count, count), 1)
    earlier = ((row // per == column // per) & (row < column)).astype(F32).astype(BF16)
    before = dot(named.astype(F32).astype(BF16), earlier)
    rank = jnp.sum(jnp.where(named, before, 0.0), axis=0, keepdims=True)
    return codes, rank.astype(jnp.int32)


def code_of(core, turn):
    return turn * CORES + (core if turn % 2 == 0 else CORES - 1 - core)


def requests_kernel(per, cap, turns, packed_ref, *list_refs):
    peers = lax.axis_size("ctx")
    codes, rank = ranks(packed_ref[...], per)
    place = (iota(codes.shape, 1) // per) * cap + rank
    parts = hi_lo(packed_ref[...] & 65535)
    length = peers * cap
    for turn in range(turns):
        code = code_of(lax.axis_index("ctx") % CORES, turn)
        wanted = jnp.where(codes == code, place, -1)
        chosen = (iota((length, codes.shape[1]), 0) == wanted).astype(F32).astype(BF16)
        packed = lax.dot_general(parts, chosen, NT, preferred_element_type=F32)
        packed = packed[0:1] * 256.0 + packed[1:2]
        list_refs[turn][...] = packed.astype(jnp.int32)


def hold_kernel(table_ref, held_ref, done_ref):
    done_ref[...] = jnp.zeros_like(done_ref)
    held_ref[...] = table_ref[...]


def places_kernel(per, cap, turns, packed_ref, rows_ref, w_in_ref, places_ref, held_ref):
    del rows_ref
    held_ref[...] = w_in_ref[...]
    peers = lax.axis_size("ctx")
    me = lax.axis_index("ctx")
    codes, rank = ranks(packed_ref[...], per)
    count = codes.shape[1]
    length = peers * cap
    turn = codes // CORES
    inner = codes % CORES
    core = jnp.where(turn % 2 == 0, inner, CORES - 1 - inner)
    buffer = jnp.where(core == me % CORES, 0, 1)
    place = (buffer * turns + turn) * length + (iota(codes.shape, 1) // per) * cap + rank
    row, column = iota((count, count), 0), iota((count, count), 1)
    block = row // per
    half = peers // 2
    relative = jnp.where(block < half, 2 * block, 2 * (block - half) + 1)
    source = (relative ^ me) * per + row % per
    order = (source == column).astype(F32).astype(BF16)
    found = lax.dot_general(order, hi_lo(place), NT, preferred_element_type=F32)
    found = (found[:, 0:1] * 256.0 + found[:, 1:2]).astype(jnp.int32)
    total = places_ref.shape[1]
    places_ref[...] = (iota((count, total), 1) == found).astype(F32).astype(BF16)


def lookup_kernel(turns, table_ref, done_ref, *refs):
    del done_ref
    refs[-1][...] = jnp.zeros_like(refs[-1])
    for list_ref, rows_ref in zip(refs[:turns], refs[turns:]):
        length = list_ref.shape[1]
        same = (iota((length, length), 0) == iota((length, length), 1)).astype(F32).astype(BF16)
        found = lax.dot_general(same, hi_lo(list_ref[...]), NT, preferred_element_type=F32)
        high, low = found[:, 0:1].astype(jnp.int32), found[:, 1:2].astype(jnp.int32)
        parts = table_ref.shape[0] // 256
        same_low = iota((length, 256), 1) == low
        chosen = [
            jnp.where(same_low & (high == part), 1.0, 0.0).astype(BF16) for part in range(parts)
        ]
        rows_ref[...] = dot(jnp.concatenate(chosen, axis=1), table_ref[...]).astype(BF16)


def attend_kernel(per, buffers, length_ref, places_ref, *refs):
    received, refs = refs[:buffers], refs[buffers:]
    w_in_ref, w_uq_hbm, keys_hbm, values_hbm = refs[:4]
    features_ref, normed_ref, keep_ref, near_ref, far_ref = refs[4:9]
    queries_ref, keys_ref, values_ref, w_query_ref, sems, weight_sem = refs[9:]
    heads, events, head_dim = keys_ref.shape
    width = heads * head_dim
    kept = keep_ref.shape[1]
    scale = 0.5 * head_dim ** (-0.5)
    group = min(GROUP, events)
    block = min(KEY_BLOCK, group)

    def copies(head):
        columns = pl.ds(pl.multiple_of(head * head_dim, head_dim), head_dim)
        return [
            pltpu.make_async_copy(hbm.at[:, columns], ref.at[head], sems.at[index, head])
            for index, (hbm, ref) in enumerate(((keys_hbm, keys_ref), (values_hbm, values_ref)))
        ]

    w_query_copy = pltpu.make_async_copy(
        w_uq_hbm.at[:, pl.ds(width, width)], w_query_ref, weight_sem
    )
    w_query_copy.start()

    @pl.loop(0, heads)
    def _(head):
        for copy in copies(head):
            copy.start()

    embedded = None
    start = 0
    for part_ref in received:
        rows = part_ref.shape[0]
        part = dot(places_ref[:, start : start + rows], part_ref[...])
        embedded = part if embedded is None else embedded + part
        start += rows
    features = dot(embedded.astype(BF16), w_in_ref[...]).astype(BF16)
    features_ref[...] = features[:per]
    normed = layer_norm(features.astype(F32)).astype(BF16)
    normed_ref[...] = normed[:per]
    w_query_copy.wait()
    together = 4
    for first in range(0, heads, together):
        columns = slice(first * head_dim, (first + together) * head_dim)
        queries = silu(dot(normed, w_query_ref[:, columns])).astype(BF16)
        for index in range(together):
            part = slice(index * head_dim, (index + 1) * head_dim)
            queries_ref[first + index] = queries[:, part]

    valid = length_ref[0] - lax.axis_index("ctx") * events

    def add_group(head, first, total, masked):
        def weights_of(start):
            keys = keys_ref[head, pl.ds(start, block), :]
            half = lax.dot_general(queries_ref[head], keys, NT, preferred_element_type=F32) * scale
            return (half + half * jnp.tanh(half)).astype(BF16)

        def values_of(start):
            values = values_ref[head, pl.ds(start, block), :]
            if masked:
                inside = (iota((block, head_dim), 0) + start) < valid
                values = jnp.where(inside, values.astype(F32), 0.0).astype(BF16)
            return values

        waiting = []
        for inner in range(group // block):
            start = first + inner * block
            if not isinstance(start, int):
                start = pl.multiple_of(start, block)
            waiting.append((weights_of(start), start))
            if len(waiting) > 0:
                weights, before = waiting.pop(0)
                total = total + dot(weights, values_of(before))
        for weights, before in waiting:
            total = total + dot(weights, values_of(before))
        return total

    def store(head, total):
        keep_ref[head] = total[:kept]
        near_ref[head] = total[kept : kept + per].astype(BF16)
        far_ref[head] = total[kept + per :].astype(BF16)

    zero = jnp.zeros((queries_ref.shape[1], head_dim), F32)

    @pl.when(valid > events - group)
    def _():
        @pl.loop(0, heads // 4)
        def _(head):
            for extra in range(4):
                one = 4 * head + extra
                if extra % 2 == 0:
                    for copy in copies(one) + copies(one + 1):
                        copy.wait()
                total = zero
                for first in range(0, events, group):
                    total = add_group(one, first, total, first + group >= events)
                store(one, total)

    @pl.when(valid <= events - group)
    def _():
        trips = jnp.maximum(valid + group - 1, 0) // group

        @pl.loop(0, heads)
        def _(head):
            for copy in copies(head):
                copy.wait()
            store(
                head,
                lax.fori_loop(0, trips, lambda i, t: add_group(head, i * group, t, True), zero),
            )


def gate_kernel(normed_ref, w_uq_ref, keep_ref, near_ref, gate_ref, base_ref):
    gate_ref[...] = silu(dot(normed_ref[...], w_uq_ref[...])).astype(BF16)
    base_ref[...] = keep_ref[...] + near_ref[...].astype(F32)


def finish_kernel(others, *refs):
    keep_ref = refs[0]
    gate_ref, features_ref, w_out_ref, out_ref = refs[1 + others :]
    parts = []
    for head in range(keep_ref.shape[0]):
        part = keep_ref[head]
        for other in refs[1 : 1 + others]:
            part = part + other[head].astype(F32)
        parts.append(part)
    attended = jnp.concatenate(parts, axis=1)
    mixed = (layer_norm(attended) * gate_ref[...].astype(F32)).astype(BF16)
    ranked = features_ref[...].astype(F32) + dot(mixed, w_out_ref[...])
    out_ref[...] = ranked.astype(BF16)


def shards(item_table, cand_owner, cand_slot, w_in, w_uq, w_out, k_cache, v_cache, hist_len):
    users, peers = lax.axis_size("req"), lax.axis_size("ctx")
    count = cand_owner.shape[1]
    per = count // peers
    cap = max(2, 2 * per // users)
    turns = users // CORES
    length = peers * cap
    width = w_out.shape[0]
    shape = jax.ShapeDtypeStruct

    def permute(values, target):
        pairs = []
        for user in range(users):
            for peer in range(peers):
                to_user, to_peer = target(user, peer)
                pairs.append((user * peers + peer, to_user * peers + to_peer))
        return lax.ppermute(values, ("req", "ctx"), pairs)

    def swap_owner(values, turn):
        return permute(values, lambda user, peer: (user ^ (users - 1) ^ code_of(peer % CORES, turn), peer))

    def swap_peer(values, step):
        return permute(values, lambda user, peer: (user, peer ^ step))

    packed = (cand_owner[:, :, 0] << 16) | cand_slot
    lists = pl.pallas_call(
        functools.partial(requests_kernel, per, cap, turns),
        in_specs=[VMEM],
        out_specs=[VMEM] * turns,
        out_shape=[shape((1, length), jnp.int32)] * turns,
        compiler_params=params(16),
        name="requests",
    )(packed)
    asked = [swap_owner(lists[turn], turn) for turn in reversed(range(turns))][::-1]
    table, table_done = pl.pallas_call(
        hold_kernel,
        in_specs=[VMEM],
        out_specs=[VMEM] * 2,
        out_shape=[shape(item_table.shape, BF16), shape((8, 128), BF16)],
        compiler_params=params(16),
        cost_estimate=pl.CostEstimate(flops=1 << 20, bytes_accessed=24 << 20, transcendentals=0),
        name="hold",
    )(item_table)
    looked, looked_done = [], table_done
    for group in (asked[: turns // 2], asked[turns // 2 :]):
        *found, looked_done = pl.pallas_call(
            functools.partial(lookup_kernel, len(group)),
            in_specs=[VMEM] * (2 + len(group)),
            out_specs=[VMEM] * (len(group) + 1),
            out_shape=[shape((length, item_table.shape[1]), BF16)] * len(group)
            + [shape((8, 128), BF16)],
            compiler_params=params(16),
            name="lookup",
        )(table, looked_done, *group)
        looked = looked + found
    places, w_in = pl.pallas_call(
        functools.partial(places_kernel, per, cap, turns),
        in_specs=[VMEM] * 3,
        out_specs=[VMEM] * 2,
        out_shape=[shape((count, users * length), BF16), shape(w_in.shape, BF16)],
        compiler_params=params(16),
        cost_estimate=pl.CostEstimate(flops=1 << 28, bytes_accessed=24 << 20, transcendentals=0),
        name="places",
    )(packed, looked_done, w_in)
    rows = [swap_owner(looked[turn], turn) for turn in reversed(range(turns))][::-1]
    *rows, places, w_in = lax.optimization_barrier((*rows, places, w_in))
    fetched = jnp.concatenate(rows, axis=0)
    buffers = [fetched, swap_peer(fetched, 1)]
    keys, values = k_cache[0], v_cache[0]
    events = keys.shape[0]
    head_dim = width // HEADS
    half = count // 2
    features, normed, keep, near, far = pl.pallas_call(
        functools.partial(attend_kernel, per, len(buffers)),
        in_specs=[SMEM] + [VMEM] * (1 + len(buffers)) + [VMEM] + [HBM] * 3,
        out_specs=[VMEM] * 5,
        out_shape=[
            shape((per, width), BF16),
            shape((per, width), BF16),
            shape((HEADS, half, head_dim), F32),
            shape((HEADS, per, head_dim), BF16),
            shape((HEADS, half - per, head_dim), BF16),
        ],
        scratch_shapes=[
            pltpu.VMEM((HEADS, count, head_dim), BF16),
            pltpu.VMEM((HEADS, events, head_dim), BF16),
            pltpu.VMEM((HEADS, events, head_dim), BF16),
            pltpu.VMEM((width, width), BF16),
            pltpu.SemaphoreType.DMA((2, HEADS)),
            pltpu.SemaphoreType.DMA,
        ],
        compiler_params=params(47),
        name="attend",
    )(hist_len, places, *buffers, w_in, w_uq, keys, values)
    sibling = swap_peer(far, 1)
    sums = []
    for index in range(1, peers // 2):
        piece = slice((index - 1) * per, index * per)
        kept = keep[:, index * per : (index + 1) * per]
        sums.append((kept + sibling[:, piece].astype(F32)).astype(BF16))
    near, *sums = lax.optimization_barrier((near, *sums))
    others = [swap_peer(one, 2 * index) for index, one in enumerate(sums, 1)]
    near = swap_peer(near, 1)
    block = pl.BlockSpec((HEADS, per, head_dim), lambda i: (0, 0, 0))
    gate, base = pl.pallas_call(
        gate_kernel,
        grid=(1,),
        in_specs=[
            pl.BlockSpec((per, width), lambda i: (0, 0)),
            pl.BlockSpec((width, width), lambda i: (0, 0)),
            block,
            block,
        ],
        out_specs=[pl.BlockSpec((per, width), lambda i: (0, 0)), block],
        out_shape=[shape((per, width), BF16), shape((HEADS, per, head_dim), F32)],
        compiler_params=params(16),
        cost_estimate=pl.CostEstimate(flops=1 << 28, bytes_accessed=3 << 20, transcendentals=0),
        name="gate",
    )(normed, w_uq, keep, near)
    ranked = pl.pallas_call(
        functools.partial(finish_kernel, len(others)),
        grid=(1,),
        in_specs=[block] * (1 + len(others))
        + [pl.BlockSpec((per, width), lambda i: (0, 0))] * 2
        + [pl.BlockSpec((width, width), lambda i: (0, 0))],
        out_specs=pl.BlockSpec((per, width), lambda i: (0, 0)),
        out_shape=shape((per, width), BF16),
        compiler_params=params(24),
        name="finish",
    )(base, *others, gate, features, w_out)
    return ranked[None]


def solution(mesh):
    in_specs = (
        P("req", None),
        P("req", None, None),
        P("req", None),
        P(),
        P(),
        P(),
        P("req", "ctx", None),
        P("req", "ctx", None),
        P("req"),
    )
    out_specs = P("req", "ctx", None)
    return jax.shard_map(shards, mesh=mesh, in_specs=in_specs, out_specs=out_specs, check_vma=False)
```
